32 devices in a mesh: side: 2 (over y), grp: 4 (over z), cuts: 4 (over x, core).
Axes of the slice: x: 2, y: 2, z: 4, core: 2. Of those that a mesh axis runs over, the one named last changes fastest.
Arguments:
- query: bfloat16 [128, 6144], P(('side', 'grp', 'cuts')), may hold values from -21 to 21, as said below
- k_cache: bfloat16 [128, 256, 1024], P(('side', 'grp', 'cuts')), may hold values from -5 to 5
- v_cache: bfloat16 [128, 256, 1024], P(('side', 'grp', 'cuts')), may hold values from -6 to 6
- new_key: bfloat16 [128, 1024], P(('side', 'grp', 'cuts')), may hold values from -6 to 6
- new_value: bfloat16 [128, 1024], P(('side', 'grp', 'cuts')), may hold values from -6 to 6
- lengths: int32 [128], P(('side', 'grp', 'cuts')), may hold values from 2 to 256, as said below
- residual: bfloat16 [128, 6144], P(('side', 'grp', 'cuts')), may hold values from -6 to 6
- norm_gain: bfloat16 [6144], replicated, may hold values from 0.099609375 to 1.8984375
- router: bfloat16 [6144, 4], replicated, may hold values from -0.078125 to 0.078125
- routes: int32 [128, 2], P(('side', 'grp', 'cuts')), may hold values from 0 to 3, all different within a row; in each aligned block of 4 rows (0 to 3, 4 to 7, ...) at most 2 rows name the same one
- w_gate: bfloat16 [4, 6144, 8192], P('grp', None, ('side', 'cuts')), may hold values from -0.078125 to 0.078125
- w_up: bfloat16 [4, 6144, 8192], P('grp', None, ('side', 'cuts')), may hold values from -0.078125 to 0.078125
- w_down: bfloat16 [4, 8192, 6144], P('grp', ('side', 'cuts')), may hold values from -0.0625 to 0.0625
Outputs:
- layer_out: bfloat16 [128, 6144], P(('side', 'grp', 'cuts'))
The draws below stay inside these ranges and needn't reach their ends.
Inputs may be any that keep to these rules, and one draw needn't show every extreme that they name: `query`: queries are the new token's queries; in some draws a few rows have queries aligned with some cached keys. `lengths`: some row in every draw has all 256 positions live. `routes`: the two experts of a row differ. Within the rows of one device (aligned blocks of 4 rows) no expert is named more than 2 times, a bound that some block of every draw reaches.
All inputs are finite; a program needn't handle non-finite values.
Results may differ from the reference program's by a relative error of at most 0.0095.
Values may be sent and summed in bfloat16 or wider, within the bound.
No kernel may reach another device: no remote copies, remote signals or barrier semaphores. Data moves between devices by JAX's collectives and lax.ppermute only.
A program may use at most 128 MiB of HBM per device.

```python
import math
import jax
import jax.numpy as jnp
import numpy as np
from jax import lax

Q_HEADS = 48
KV_HEADS = 8
HEAD_DIM = 128
D = 6144
FF = 8192
ROW_DEV = 4
SPAN = 256
EXPERTS = 4
MOST = 2
ROWS = 128
N_SIDE = 2
N_CUTS = 4


def draw_query(key, part):
    own = jax.random.fold_in(key, 21)
    return jnp.clip(jax.random.normal(own, (ROWS, D), jnp.float32), -4.5, 4.5).astype(jnp.bfloat16)


def draw_k_cache(key, part):
    own = jax.random.fold_in(key, 22)
    return jnp.clip(jax.random.normal(own, (ROWS, SPAN, KV_HEADS * HEAD_DIM), jnp.float32), -4.5, 4.5).astype(jnp.bfloat16)


def draw_lengths(key, part):
    lowest = max(2, SPAN // 8)
    drawn = jax.random.randint(jax.random.fold_in(key, 31), (ROWS,), lowest, SPAN + 1)
    filled = jax.random.randint(jax.random.fold_in(key, 32), (), 0, ROWS)
    return jnp.where(jnp.arange(ROWS) == filled, SPAN, drawn).astype(jnp.int32)


def level_of(rng, shape, pieces, smallest, top_value):
    factor_of, own = 1.0, jax.random.fold_in(rng, 6)
    for position, parts in pieces:
        heights = jnp.exp(jax.random.uniform(jax.random.fold_in(own, position), (parts,), jnp.float32, smallest / len(pieces), top_value / len(pieces)))
        factor_of = factor_of * jnp.repeat(heights, shape[position] // parts).reshape([-1 if axis == position else 1 for axis in range(len(shape))])
    return factor_of


def shared_out(key, own, number, rows, count, top, limit, slope):
    ranking = jax.random.permutation(key, count)
    crowded, common = load_shares(count, rows * top, limit, slope, True), load_shares(count, rows * top, limit, slope, False)
    places = jnp.arange(count)

    def named(sizes, turn):
        used = int((sizes > 0).sum())
        fixed = max(1, used // 4)
        shifted = fixed + (places - fixed + turn * (used - fixed)) % max(1, count - fixed)
        return jnp.zeros((count,), jnp.int32).at[ranking[jnp.where(places < fixed, places, shifted)]].set(jnp.asarray(sizes, jnp.int32))

    sizes = jnp.where(number % 4 == 0, named(crowded, number // 4), named(common, number - number // 4 - 1))
    mixed = jax.random.permutation(jax.random.fold_in(own, 3), count)
    source_of, taker = mixed[0:count // 2 * 2:2], mixed[1:count // 2 * 2:2]
    margin = jnp.minimum(sizes[source_of] - 1, limit - sizes[taker]) // 2
    margin = jnp.where((source_of == ranking[0]) | (taker == ranking[0]) | (sizes[taker] == 0), 0, jnp.maximum(margin, 0))
    shifted = jax.random.randint(jax.random.fold_in(own, 4), (count // 2,), 0, 1 << 20) % (margin + 1)
    sizes = sizes.at[source_of].add(-shifted).at[taker].add(shifted)
    labels = jnp.searchsorted(jnp.cumsum(sizes), jnp.arange(rows * top), side="right").astype(jnp.int32)
    listing = labels.reshape(top, rows).T
    listing = listing[jax.random.permutation(jax.random.fold_in(own, 1), rows)]
    turn = jax.random.randint(jax.random.fold_in(own, 2), (rows, 1), 0, top)
    return jnp.take_along_axis(listing, (jnp.arange(top)[None, :] + turn) % top, axis=1)


def load_shares(count, total, reach, slope, full):
    loads = [(1 << 20) // math.isqrt(rank ** slope) + 1 for rank in range(1, count + 1)]
    largest = reach if full else min(reach, max(-(-total // count), total * loads[0] // sum(loads)))
    least = 1 if total - largest >= count - 1 else 0
    given, spare = [largest] + [least] * (count - 1), total - largest - least * (count - 1)
    while spare > 0:
        movable = [i for i in range(1, count) if given[i] < largest] or [i for i in range(1, count) if given[i] < reach]
        whole, remaining = sum([loads[i] for i in movable]), spare
        for i in movable:
            more = min(reach - given[i], max(1, remaining * loads[i] // whole), spare)
            given[i] = given[i] + more
            spare = spare - more
    return np.array(given)


def normal_values(key, extent, scale, limit, split=(), kind=jnp.bfloat16):
    entries = jax.random.normal(key, extent, jnp.float32) * scale
    if len(split) > 0:
        entries = level_of(key, extent, split, -0.22, 0.18) * entries
    return jnp.clip(entries, min=-limit, max=limit).astype(kind)


def setup_inputs(seed: int = 0) -> dict:
    key_list = jax.random.split(jax.random.key(seed), 14)
    query = draw_query(jax.random.fold_in(key_list[13], 71), 0)
    k_cache = draw_k_cache(jax.random.fold_in(key_list[13], 71), 0)
    v_cache = normal_values(key_list[2], (ROWS, SPAN, KV_HEADS * HEAD_DIM), 1.0, 6.0, ((0, 32),))
    new_key = normal_values(key_list[3], (ROWS, KV_HEADS * HEAD_DIM), 1.0, 6.0, ((0, 32),))
    new_value = normal_values(key_list[4], (ROWS, KV_HEADS * HEAD_DIM), 1.0, 6.0, ((0, 32),))
    lengths = draw_lengths(jax.random.fold_in(key_list[13], 71), 0)
    residual = normal_values(key_list[6], (ROWS, D), 1.0, 6.0, ((0, 32),))
    norm_gain = jnp.clip(1.0 + 0.18 * jax.random.normal(key_list[7], (D,), jnp.float32), 0.099609375, 1.8984375).astype(jnp.bfloat16)
    router = normal_values(key_list[8], (D, EXPERTS), D ** -0.5, 0.078125)
    routes_keys = jax.random.split(jax.random.fold_in(key_list[9], 1), ROWS // ROW_DEV)
    routes_turns = jax.random.permutation(jax.random.fold_in(key_list[9], 3), ROWS // ROW_DEV)
    routes = jax.vmap(lambda own, number: shared_out(jax.random.fold_in(key_list[9], 2), own, number, ROW_DEV, EXPERTS, 2, MOST, 2))(routes_keys, routes_turns).reshape((ROWS, 2))
    w_gate = normal_values(key_list[10], (EXPERTS, D, FF), D ** -0.5, 0.078125, ((0, 4), (2, 8)))
    w_up = normal_values(key_list[11], (EXPERTS, D, FF), D ** -0.5, 0.078125, ((0, 4), (2, 8)))
    w_down = normal_values(key_list[12], (EXPERTS, FF, D), FF ** -0.5, 0.0625, ((0, 4), (1, 8)))
    return dict(query=query, k_cache=k_cache, v_cache=v_cache, new_key=new_key, new_value=new_value, lengths=lengths, residual=residual, norm_gain=norm_gain, router=router, routes=routes, w_gate=w_gate, w_up=w_up, w_down=w_down)


def attend(query, k_cache, v_cache, new_key, new_value, lengths):
    rows, span, _ = k_cache.shape
    group = Q_HEADS // KV_HEADS
    scale = 1.0 / math.sqrt(HEAD_DIM)
    queries = query.astype(jnp.float32).reshape(rows, KV_HEADS, group, HEAD_DIM)
    keys = k_cache.astype(jnp.float32).reshape(rows, span, KV_HEADS, HEAD_DIM)
    values = v_cache.astype(jnp.float32).reshape(rows, span, KV_HEADS, HEAD_DIM)
    fresh_key = new_key.astype(jnp.float32).reshape(rows, KV_HEADS, HEAD_DIM)
    fresh_value = new_value.astype(jnp.float32).reshape(rows, KV_HEADS, 1, HEAD_DIM)
    old = jnp.einsum('rkgd,rskd->rkgs', queries, keys) * scale
    own = jnp.einsum('rkgd,rkd->rkg', queries, fresh_key) * scale
    live = jnp.arange(span)[None, :] < lengths[:, None]
    old = jnp.where(live[:, None, None, :], old, -jnp.inf)
    top = jnp.maximum(lax.optimization_barrier(jnp.max(old, axis=-1)), own)
    e_old = jnp.exp(old - top[..., None])
    e_own = jnp.exp(own - top)
    total = lax.optimization_barrier(jnp.sum(e_old, axis=-1)) + e_own
    p_old = (e_old / total[..., None]).astype(jnp.bfloat16).astype(jnp.float32)
    p_own = (e_own / total).astype(jnp.bfloat16).astype(jnp.float32)
    out = jnp.einsum('rkgs,rskd->rkgd', p_old, values) + p_own[..., None] * fresh_value
    return out.reshape(rows, Q_HEADS * HEAD_DIM)

def slot_ranks(block):
    flat = block.reshape(-1)
    order = jnp.arange(flat.shape[0])
    same = (flat[:, None] == flat[None, :]) & (order[None, :] < order[:, None])
    return lax.optimization_barrier(jnp.sum(same.astype(jnp.int32), axis=1)).reshape(block.shape)

def reference(query, k_cache, v_cache, new_key, new_value, lengths, residual, norm_gain, router, routes, w_gate, w_up, w_down):
    attended = attend(query, k_cache, v_cache, new_key, new_value, lengths)
    mixed = residual.astype(jnp.float32) + attended
    power = lax.optimization_barrier(jnp.mean(mixed * mixed, axis=1, keepdims=True))
    normed = (mixed * lax.rsqrt(power + 1e-05) * norm_gain.astype(jnp.float32)).astype(jnp.bfloat16)
    logits = jnp.dot(normed, router, preferred_element_type=jnp.float32)
    picked = jnp.take_along_axis(logits, routes, axis=1)
    first = jax.nn.sigmoid(picked[:, 0] - picked[:, 1])
    second = jax.nn.sigmoid(picked[:, 1] - picked[:, 0])
    blocks_count = ROWS // ROW_DEV
    blocks = routes.reshape(blocks_count, ROW_DEV, 2)
    ranks = jax.vmap(slot_ranks)(blocks)
    normed_blocks = normed.reshape(blocks_count, ROW_DEV, D).astype(jnp.float32)
    slot_ids = jnp.arange(MOST).astype(jnp.int32)
    slices = N_SIDE * N_CUTS
    slice_width = FF // slices

    def one_expert(item):
        expert_id, gate_w, up_w, down_w = item
        match = (blocks == expert_id)[:, None] & (ranks[:, None] == slot_ids[None, :, None, None])
        pick = lax.optimization_barrier(jnp.sum(match.astype(jnp.float32), axis=-1))
        buffer = jnp.einsum('bmr,brx->bmx', pick, normed_blocks).astype(jnp.bfloat16).reshape(blocks_count * MOST, D)
        gate = jnp.dot(buffer, gate_w, preferred_element_type=jnp.float32)
        upper = jnp.dot(buffer, up_w, preferred_element_type=jnp.float32)
        act = (jax.nn.silu(gate) * upper).astype(jnp.bfloat16)
        summed = jnp.zeros((blocks_count * MOST, D), jnp.float32)
        for index in range(slices):
            low = index * slice_width
            piece = jnp.dot(act[:, low:low + slice_width], down_w[low:low + slice_width], preferred_element_type=jnp.float32)
            piece = lax.optimization_barrier(piece.astype(jnp.bfloat16))
            summed = summed + piece.astype(jnp.float32)
        return summed
    expert_ids = jnp.arange(EXPERTS).astype(jnp.int32)
    results = lax.map(one_expert, (expert_ids, w_gate, w_up, w_down))
    owner = (jnp.arange(ROWS) // ROW_DEV).astype(jnp.int32)
    slot_index = (owner[:, None] * MOST + ranks.reshape(ROWS, 2)).astype(jnp.int32)
    taken = results[routes, slot_index]
    total = mixed + first[:, None] * taken[:, 0] + second[:, None] * taken[:, 1]
    return total.astype(jnp.bfloat16)
```

```python
import math

import jax
import jax.numpy as jnp
from jax import lax
from jax.sharding import PartitionSpec as P

Q_HEADS = 48
KV_HEADS = 8
HEAD_DIM = 128


def attend(query, k_cache, v_cache, new_key, new_value, lengths):
    rows, span, _ = k_cache.shape
    group = Q_HEADS // KV_HEADS
    scale = 1.0 / math.sqrt(HEAD_DIM)
    queries = query.reshape(rows, KV_HEADS, group, HEAD_DIM)
    keys = k_cache.reshape(rows, span, KV_HEADS, HEAD_DIM)
    values = v_cache.reshape(rows, span, KV_HEADS, HEAD_DIM)
    fresh_key = new_key.reshape(rows, KV_HEADS, HEAD_DIM)
    fresh_value = new_value.astype(jnp.float32).reshape(rows, KV_HEADS, 1, HEAD_DIM)
    old = jnp.einsum("rkgd,rskd->rkgs", queries, keys, preferred_element_type=jnp.float32) * scale
    own = (
        jnp.einsum("rkgd,rkd->rkg", queries, fresh_key, preferred_element_type=jnp.float32) * scale
    )
    live = jnp.arange(span)[None, :] < lengths[:, None]
    old = jnp.where(live[:, None, None, :], old, -jnp.inf)
    top = jnp.maximum(jnp.max(old, axis=-1), own)
    e_old = jnp.exp(old - top[..., None])
    e_own = jnp.exp(own - top)
    total = jnp.sum(e_old, axis=-1) + e_own
    p_old = (e_old / total[..., None]).astype(jnp.bfloat16)
    p_own = (e_own / total).astype(jnp.bfloat16).astype(jnp.float32)
    out = jnp.einsum("rkgs,rskd->rkgd", p_old, values, preferred_element_type=jnp.float32)
    out = out + p_own[..., None] * fresh_value
    return out.reshape(rows, Q_HEADS * HEAD_DIM)


def slot_ranks(block):
    flat = block.reshape(-1)
    order = jnp.arange(flat.shape[0])
    same = (flat[:, None] == flat[None, :]) & (order[None, :] < order[:, None])
    return jnp.sum(same.astype(jnp.int32), axis=1).reshape(block.shape)


def activate(rows_in, gate_w, up_w):
    gate = jnp.dot(rows_in, gate_w, preferred_element_type=jnp.float32)
    upper = jnp.dot(rows_in, up_w, preferred_element_type=jnp.float32)
    return (jax.nn.silu(gate) * upper).astype(jnp.bfloat16)


def local(
    query,
    k_cache,
    v_cache,
    new_key,
    new_value,
    lengths,
    residual,
    norm_gain,
    router,
    routes,
    w_gate,
    w_up,
    w_down,
):
    rows = query.shape[0]
    width = query.shape[1]
    experts = lax.axis_size("grp")
    n_side = lax.axis_size("side")
    n_cuts = lax.axis_size("cuts")
    most = max(2, 2 * rows // experts)
    gate_w = w_gate[0]
    up_w = w_up[0]
    down_w = w_down[0]
    attended = attend(query, k_cache, v_cache, new_key, new_value, lengths)
    mixed = residual.astype(jnp.float32) + attended
    power = jnp.mean(mixed * mixed, axis=1, keepdims=True)
    normed = (mixed * lax.rsqrt(power + 1e-05) * norm_gain.astype(jnp.float32)).astype(jnp.bfloat16)
    logits = jnp.dot(normed, router, preferred_element_type=jnp.float32)
    chosen = routes[:, :, None] == jnp.arange(experts)[None, None, :]
    picked = jnp.sum(jnp.where(chosen, logits[:, None, :], 0.0), axis=-1)
    first = jax.nn.sigmoid(picked[:, 0] - picked[:, 1])
    second = jax.nn.sigmoid(picked[:, 1] - picked[:, 0])
    weights = jnp.stack([first, second], axis=1)
    ranks = slot_ranks(routes)
    slot_of = routes * most + ranks
    slot_range = jnp.arange(experts * most)
    placing = slot_of[:, :, None] == slot_range[None, None, :]
    one_hot = jnp.sum(placing.astype(jnp.float32), axis=1).astype(jnp.bfloat16)
    outgoing = jnp.einsum("rj,rx->jx", one_hot, normed, preferred_element_type=jnp.float32).astype(
        jnp.bfloat16
    )
    by_expert = lax.all_to_all(outgoing, "grp", split_axis=0, concat_axis=0, tiled=True)
    arrived = lax.all_gather(by_expert, ("side", "cuts"), axis=0, tiled=True)
    hidden = activate(arrived, gate_w, up_w)
    partial = jnp.dot(hidden, down_w, preferred_element_type=jnp.float32).astype(jnp.bfloat16)
    pieces = lax.all_to_all(partial, ("side", "cuts"), split_axis=0, concat_axis=0, tiled=True)
    mine = jnp.sum(
        pieces.reshape(n_side * n_cuts, experts * most, width).astype(jnp.float32), axis=0
    )
    returned = lax.all_to_all(
        mine.astype(jnp.bfloat16), "grp", split_axis=0, concat_axis=0, tiled=True
    ).astype(jnp.float32)
    mixing = jnp.sum(jnp.where(placing, weights[:, :, None], 0.0), axis=1)
    combined = jnp.dot(
        mixing, returned, precision=lax.Precision.HIGHEST, preferred_element_type=jnp.float32
    )
    return (mixed + combined).astype(jnp.bfloat16)


def solution(mesh):
    placed = (
        P(("side", "grp", "cuts"), None),
        P(("side", "grp", "cuts"), None, None),
        P(("side", "grp", "cuts"), None, None),
        P(("side", "grp", "cuts"), None),
        P(("side", "grp", "cuts"), None),
        P(("side", "grp", "cuts")),
        P(("side", "grp", "cuts"), None),
        P(),
        P(),
        P(("side", "grp", "cuts"), None),
        P("grp", None, ("side", "cuts")),
        P("grp", None, ("side", "cuts")),
        P("grp", ("side", "cuts"), None),
    )
    return jax.shard_map(
        local,
        mesh=mesh,
        in_specs=placed,
        out_specs=P(("side", "grp", "cuts"), None),
        check_vma=False,
    )
```

```python
import functools
import math

import jax
import jax.numpy as jnp
from jax import lax
from jax.experimental import pallas as pl
from jax.experimental.pallas import tpu as pltpu
from jax.sharding import PartitionSpec as P

Q_HEADS = 48
KV_HEADS = 8
HEAD_DIM = 128
GROUP = Q_HEADS // KV_HEADS
MIB = 2**20
VMEM = pl.BlockSpec(memory_space=pltpu.VMEM)
SMEM = pl.BlockSpec(memory_space=pltpu.SMEM)
HBM = pl.BlockSpec(memory_space=pltpu.HBM)
ANY = pl.BlockSpec(memory_space=pl.ANY)


def stacked_heads(x, first, copies=1):
    parts = [x[:, (first + j) * HEAD_DIM : (first + j + 1) * HEAD_DIM] for j in range(GROUP // copies)]
    return jnp.concatenate(parts * copies, axis=0)


def attend_kernel(experts, most, n_in, *refs):
    hbm_refs = refs[:n_in]
    out_refs = refs[n_in : n_in + experts]
    mixed_ref, mixing_ref = refs[n_in + experts : n_in + experts + 2]
    scratch = refs[n_in + experts + 2 : -2]
    sem, cache_sems = refs[-2:]
    k_any, v_any = hbm_refs[-2:]
    k_ref, v_ref = scratch[-2:]
    lengths, routes, q_ref, nk_ref, nv_ref, res_ref, gain_ref, router_ref = scratch[:-2]
    rows, width = q_ref.shape
    span = k_ref.shape[1]
    scale = 1.0 / math.sqrt(HEAD_DIM)
    small = [
        pltpu.make_async_copy(hbm_refs[i], scratch[i], sem.at[i]) for i in range(n_in - 2)
    ]
    loads_k = [
        pltpu.make_async_copy(k_any.at[r], k_ref.at[r], cache_sems.at[0, r]) for r in range(rows)
    ]
    loads_v = [
        pltpu.make_async_copy(v_any.at[r], v_ref.at[r], cache_sems.at[1, r]) for r in range(rows)
    ]
    for load in small + loads_k + loads_v:
        load.start()
    for load in small:
        load.wait()

    pair = 2
    pairs = KV_HEADS // pair
    stack = GROUP * rows
    tall = pair * stack
    wide = pair * HEAD_DIM
    row_of = lax.broadcasted_iota(jnp.int32, (tall, 1), 0) % rows
    length_of = jnp.zeros((tall, 1), jnp.int32)
    for r in range(rows):
        length_of = jnp.where(row_of == r, lengths[r], length_of)
    live = lax.broadcasted_iota(jnp.int32, (tall, span), 1) < length_of

    query = q_ref[...].astype(jnp.float32)
    new_key = nk_ref[...].astype(jnp.float32)
    new_value = nv_ref[...].astype(jnp.float32)
    blank = jnp.zeros((stack, HEAD_DIM), jnp.float32)
    lhs, own = [], []
    for p in range(pairs):
        heads = [stacked_heads(query, (pair * p + a) * GROUP) for a in range(pair)]
        keys = [stacked_heads(new_key, pair * p + a, GROUP) for a in range(pair)]
        lhs.append(
            jnp.concatenate(
                [
                    jnp.concatenate([heads[b] if a == b else blank for b in range(pair)], axis=1)
                    for a in range(pair)
                ],
                axis=0,
            ).astype(jnp.bfloat16)
        )
        own.append(
            jnp.sum(
                jnp.concatenate(heads, axis=0) * jnp.concatenate(keys, axis=0),
                axis=1,
                keepdims=True,
            )
            * scale
        )

    scores = [None] * pairs
    for r in range(rows):
        loads_k[r].wait()
        for p in range(pairs):
            part = lax.dot_general(
                lhs[p],
                k_ref[r, :, p * wide : (p + 1) * wide],
                (((1,), (1,)), ((), ())),
                preferred_element_type=jnp.float32,
            )
            scores[p] = part if r == 0 else jnp.where(row_of == r, part, scores[p])
    probs, own_probs = [], []
    for p in range(pairs):
        old = jnp.where(live, scores[p] * scale, -1e30)
        top = jnp.maximum(jnp.max(old, axis=1, keepdims=True), own[p])
        e_old = jnp.exp(old - top)
        e_own = jnp.exp(own[p] - top)
        share = 1.0 / (jnp.sum(e_old, axis=1, keepdims=True) + e_own)
        probs.append((e_old * share).astype(jnp.bfloat16))
        own_probs.append((e_own * share).astype(jnp.bfloat16).astype(jnp.float32))
    sums = [None] * pairs
    for r in range(rows):
        loads_v[r].wait()
        for p in range(pairs):
            part = jnp.dot(
                probs[p],
                v_ref[r, :, p * wide : (p + 1) * wide],
                preferred_element_type=jnp.float32,
            )
            sums[p] = part if r == 0 else jnp.where(row_of == r, part, sums[p])
    power = jnp.zeros((rows, HEAD_DIM), jnp.float32)
    for p in range(pairs):
        for a in range(pair):
            head = pair * p + a
            fresh = stacked_heads(new_value, head, GROUP)
            low = a * stack
            attended = (
                sums[p][low : low + stack, a * HEAD_DIM : (a + 1) * HEAD_DIM]
                + own_probs[p][low : low + stack] * fresh
            )
            for j in range(GROUP):
                at = pl.ds((head * GROUP + j) * HEAD_DIM, HEAD_DIM)
                mixed = res_ref[:, at].astype(jnp.float32) + attended[j * rows : (j + 1) * rows]
                mixed_ref[:, at] = mixed
                power = power + mixed * mixed
    mean = jnp.sum(power, axis=1, keepdims=True) * (1.0 / width)
    normed = mixed_ref[...] * lax.rsqrt(mean + 1e-05) * gain_ref[...].astype(jnp.float32).reshape(1, width)
    normed = normed.astype(jnp.bfloat16).astype(jnp.float32)

    router = router_ref[...].astype(jnp.float32)
    logits = [jnp.sum(normed * router[e : e + 1], axis=1, keepdims=True) for e in range(experts)]
    row_col = lax.broadcasted_iota(jnp.int32, (rows, 1), 0)

    def picked(i):
        value = jnp.zeros((rows, 1), jnp.float32)
        for r in range(rows):
            for e in range(experts):
                value = jnp.where((row_col == r) & (routes[i, r] == e), logits[e], value)
        return value

    first, second = picked(0), picked(1)
    share_of = [1.0 / (1.0 + jnp.exp(second - first)), 1.0 / (1.0 + jnp.exp(first - second))]

    here = lax.axis_index("grp")
    named = [(r, i, routes[i, r]) for r in range(rows) for i in range(2)]
    slots = []
    for at, (r, i, e) in enumerate(named):
        rank = jnp.int32(0)
        for _, _, other in named[:at]:
            rank = rank + (other == e).astype(jnp.int32)
        slots.append(jnp.bitwise_xor(e, here) * most + rank)
    slot_col = lax.broadcasted_iota(jnp.int32, (experts * most, 1), 0)
    slot_row = lax.broadcasted_iota(jnp.int32, (rows, experts * most), 1)
    outgoing = jnp.zeros((experts * most, width), jnp.float32)
    mixing = jnp.zeros((rows, experts * most), jnp.float32)
    for (r, i, _), slot in zip(named, slots, strict=True):
        outgoing = jnp.where(slot_col == slot, normed[r : r + 1], outgoing)
        mixing = jnp.where((slot_row == slot) & (row_col == r), share_of[i], mixing)
    outgoing = outgoing.astype(jnp.bfloat16)
    for j in range(experts):
        out_refs[j][...] = outgoing[j * most : (j + 1) * most]
    mixing_ref[...] = mixing


def load_kernel(w_ref, _, out_ref, sem):
    load = pltpu.make_async_copy(w_ref.at[0], out_ref, sem)
    load.start()
    load.wait()


def stack_kernel(*refs):
    refs[-1][...] = jnp.concatenate(
        [ref[...].astype(jnp.float32) for ref in refs[:-2]], axis=0
    ).astype(jnp.bfloat16)


def experts_kernel(
    own_ref,
    rest_ref,
    core_own_ref,
    core_rest_ref,
    gate_ref,
    up_ref,
    down_any,
    keep_ref,
    send_ref,
    x_ref,
    gate_sum,
    up_sum,
    down_ref,
    sems,
):
    loads = []
    wide = down_ref.shape[1] // sems.shape[0]
    for i in range(sems.shape[0]):
        at = pl.ds(i * wide, wide)
        loads.append(
            pltpu.make_async_copy(down_any.at[0, :, at], down_ref.at[:, at], sems.at[i])
        )
        loads[-1].start()
    width = x_ref.shape[1]
    half = keep_ref.shape[0]
    x_ref[:half] = jnp.concatenate([own_ref[...], rest_ref[...]], axis=0)
    x_ref[half:] = jnp.concatenate([core_own_ref[...], core_rest_ref[...]], axis=0)
    deep = 1024
    for step in range(width // deep):
        at = pl.ds(step * deep, deep)
        x = x_ref[:, at]
        gate = jnp.dot(x, gate_ref[at, :], preferred_element_type=jnp.float32)
        upper = jnp.dot(x, up_ref[at, :], preferred_element_type=jnp.float32)
        if step == 0:
            gate_sum[...] = gate
            up_sum[...] = upper
        else:
            gate_sum[...] += gate
            up_sum[...] += upper
    gate = gate_sum[...]
    hidden = (gate / (1.0 + jnp.exp(-gate)) * up_sum[...]).astype(jnp.bfloat16)
    for i, load in enumerate(loads):
        load.wait()
        for low in range(i * wide, (i + 1) * wide, deep):
            at = pl.ds(low, deep)
            piece = jnp.dot(hidden, down_ref[:, at], preferred_element_type=jnp.float32)
            piece = piece.astype(jnp.bfloat16)
            keep_ref[:, at] = piece[:half]
            send_ref[:, at] = piece[half:]


def chip_sum_kernel(keep_ref, got_ref, own_ref, *out_refs):
    total = keep_ref[...].astype(jnp.float32) + got_ref[...].astype(jnp.float32)
    part = own_ref.shape[0]
    own_ref[...] = total[:part]
    for i, ref in enumerate(out_refs):
        ref[...] = total[(i + 1) * part : (i + 2) * part].astype(jnp.bfloat16)


def plane_sum_kernel(got, own_ref, *refs):
    total = own_ref[...]
    for ref in refs[:got]:
        total = total + ref[...].astype(jnp.float32)
    total = total.astype(jnp.bfloat16)
    outs = refs[got:]
    most = outs[0].shape[0]
    for j, ref in enumerate(outs):
        ref[...] = total[j * most : (j + 1) * most]


def finish_kernel(mixed_ref, mixing_ref, *refs):
    total = mixed_ref[...]
    most = refs[0].shape[0]
    for j, ref in enumerate(refs[:-1]):
        rows = ref[...].astype(jnp.float32)
        for s in range(most):
            at = j * most + s
            total = total + mixing_ref[:, at : at + 1] * rows[s : s + 1]
    refs[-1][...] = total.astype(jnp.bfloat16)


def call(kernel, outs, in_specs, *args, scratch=(), limit=8, cost=None):
    return pl.pallas_call(
        kernel,
        out_shape=outs,
        in_specs=in_specs,
        out_specs=jax.tree.map(lambda _: VMEM, outs),
        scratch_shapes=list(scratch),
        compiler_params=pltpu.CompilerParams(vmem_limit_bytes=limit * MIB),
        cost_estimate=cost,
    )(*args)


def in_hbm(x):
    return pltpu.with_memory_space_constraint(x, pltpu.HBM)


def shape(extent, kind=jnp.bfloat16):
    return jax.ShapeDtypeStruct(extent, kind)


def local(
    query,
    k_cache,
    v_cache,
    new_key,
    new_value,
    lengths,
    residual,
    norm_gain,
    router,
    routes,
    w_gate,
    w_up,
    w_down,
):
    rows, width = query.shape
    experts = lax.axis_size("grp")
    n_side = lax.axis_size("side")
    n_cuts = lax.axis_size("cuts")
    most = max(2, 2 * rows // experts)
    slots = experts * most
    plane = ("side", "cuts")

    def to_grp(x, j):
        return lax.ppermute(x, "grp", [(i, i ^ j) for i in range(experts)])

    def to_plane(x, k):
        return lax.ppermute(x, plane, [(i, i ^ k) for i in range(n_side * n_cuts)])

    small = [
        lengths,
        routes.T,
        query,
        new_key,
        new_value,
        residual,
        norm_gain,
        router.T,
    ]
    *outgoing, mixed, mixing = call(
        functools.partial(attend_kernel, experts, most, len(small) + 2),
        [shape((most, width)) for _ in range(experts)]
        + [shape((rows, width), jnp.float32), shape((rows, slots), jnp.float32)],
        [HBM] * (len(small) + 2),
        *[in_hbm(x) for x in small],
        in_hbm(k_cache),
        in_hbm(v_cache),
        scratch=[
            (pltpu.SMEM if i < 2 else pltpu.VMEM)(x.shape, x.dtype) for i, x in enumerate(small)
        ]
        + [
            pltpu.VMEM(k_cache.shape, jnp.bfloat16),
            pltpu.VMEM(v_cache.shape, jnp.bfloat16),
            pltpu.SemaphoreType.DMA((len(small),)),
            pltpu.SemaphoreType.DMA((2, rows)),
        ],
        limit=14,
    )

    def load(weights, after):
        extent = weights.shape[1:]
        return call(
            load_kernel,
            pltpu.VMEM(extent, jnp.bfloat16),
            [HBM, ANY],
            in_hbm(weights),
            after,
            scratch=[pltpu.SemaphoreType.DMA],
            cost=pl.CostEstimate(
                flops=0, bytes_accessed=math.prod(extent) * 2, transcendentals=0
            ),
        )

    gate = load(w_gate, mixing)
    arrived = [outgoing[0]] + [to_grp(outgoing[j], j) for j in range(1, experts)]
    block = call(stack_kernel, shape((slots, width)), [VMEM] * experts + [ANY], *arrived, gate)
    upper = load(w_up, block)
    chips = range(0, n_side * n_cuts, 2)
    others = len(chips) - 1
    fetched = [to_plane(block, k) for k in chips[1:]]
    rest = call(
        stack_kernel, shape((others * slots, width)), [VMEM] * others + [ANY], *fetched, upper
    )
    parts = [block, rest, to_plane(block, 1), to_plane(rest, 1)]
    half = len(chips) * slots
    hidden = w_gate.shape[2]
    keep, send = call(
        experts_kernel,
        [shape((half, width))] * 2,
        [VMEM] * 6 + [HBM],
        *parts,
        gate,
        upper,
        in_hbm(w_down),
        scratch=[
            pltpu.VMEM((2 * half, width), jnp.bfloat16),
            pltpu.VMEM((2 * half, hidden), jnp.float32),
            pltpu.VMEM((2 * half, hidden), jnp.float32),
            pltpu.VMEM((hidden, width), jnp.bfloat16),
            pltpu.SemaphoreType.DMA((3,)),
        ],
        limit=24,
    )
    got = to_plane(send, 1)
    own, *partial = call(
        chip_sum_kernel,
        [shape((slots, width), jnp.float32)] + [shape((slots, width))] * others,
        [VMEM] * 2,
        keep,
        got,
    )
    gathered = [to_plane(x, k) for x, k in zip(partial, chips[1:], strict=True)]
    finished = call(
        functools.partial(plane_sum_kernel, len(gathered)),
        [shape((most, width)) for _ in range(experts)],
        [VMEM] * (1 + len(gathered)),
        own,
        *gathered,
    )
    returned = [finished[0]] + [to_grp(finished[j], j) for j in range(1, experts)]
    return call(
        finish_kernel,
        shape((rows, width)),
        [VMEM] * (2 + experts),
        mixed,
        mixing,
        *returned,
    )


def solution(mesh):
    placed = (
        P(("side", "grp", "cuts"), None),
        P(("side", "grp", "cuts"), None, None),
        P(("side", "grp", "cuts"), None, None),
        P(("side", "grp", "cuts"), None),
        P(("side", "grp", "cuts"), None),
        P(("side", "grp", "cuts")),
        P(("side", "grp", "cuts"), None),
        P(),
        P(),
        P(("side", "grp", "cuts"), None),
        P("grp", None, ("side", "cuts")),
        P("grp", None, ("side", "cuts")),
        P("grp", ("side", "cuts"), None),
    )
    return jax.shard_map(
        local,
        mesh=mesh,
        in_specs=placed,
        out_specs=P(("side", "grp", "cuts"), None),
        check_vma=False,
    )
```

```python
import functools
import math

import jax
import jax.numpy as jnp
from jax import lax
from jax.experimental import pallas as pl
from jax.experimental.pallas import tpu as pltpu
from jax.sharding import PartitionSpec as P

Q_HEADS = 48
KV_HEADS = 8
HEAD_DIM = 128
GROUP = Q_HEADS // KV_HEADS
MIB = 2**20
VMEM = pl.BlockSpec(memory_space=pltpu.VMEM)
SMEM = pl.BlockSpec(memory_space=pltpu.SMEM)
HBM = pl.BlockSpec(memory_space=pltpu.HBM)
ANY = pl.BlockSpec(memory_space=pl.ANY)


def stacked_heads(x, first, copies=1):
    parts = [x[:, (first + j) * HEAD_DIM : (first + j + 1) * HEAD_DIM] for j in range(GROUP // copies)]
    return jnp.concatenate(parts * copies, axis=0)


def attend_kernel(experts, most, n_in, *refs):
    hbm_refs = refs[:n_in]
    out_refs = refs[n_in : n_in + experts]
    mixed_ref, mixing_ref = refs[n_in + experts : n_in + experts + 2]
    scratch = refs[n_in + experts + 2 : -2]
    sem, cache_sems = refs[-2:]
    k_any, v_any = hbm_refs[-2:]
    k_ref, v_ref = scratch[-2:]
    lengths, routes, q_ref, nk_ref, nv_ref, res_ref, gain_ref, router_ref = scratch[:-2]
    rows, width = q_ref.shape
    span = k_ref.shape[1]
    scale = 1.0 / math.sqrt(HEAD_DIM)
    small = [
        pltpu.make_async_copy(hbm_refs[i], scratch[i], sem.at[i]) for i in range(n_in - 2)
    ]

    def load_k(r):
        return pltpu.make_async_copy(k_any.at[r], k_ref.at[r], cache_sems.at[0, r])

    def load_v(r):
        return pltpu.make_async_copy(v_any.at[r], v_ref.at[r], cache_sems.at[1, r])

    for load in small:
        load.start()

    @pl.loop(0, rows)
    def _(r):
        load_k(r).start()

    @pl.loop(0, rows)
    def _(r):
        load_v(r).start()

    for load in small:
        load.wait()

    pair = 2
    pairs = KV_HEADS // pair
    stack = GROUP * rows
    tall = pair * stack
    wide = pair * HEAD_DIM
    row_of = lax.broadcasted_iota(jnp.int32, (tall, 1), 0) % rows
    length_of = jnp.zeros((tall, 1), jnp.int32)
    for r in range(rows):
        length_of = jnp.where(row_of == r, lengths[r], length_of)
    live = lax.broadcasted_iota(jnp.int32, (tall, span), 1) < length_of

    query = q_ref[...].astype(jnp.float32)
    new_key = nk_ref[...].astype(jnp.float32)
    new_value = nv_ref[...].astype(jnp.float32)
    blank = jnp.zeros((stack, HEAD_DIM), jnp.float32)
    lhs, own = [], []
    for p in range(pairs):
        heads = [stacked_heads(query, (pair * p + a) * GROUP) for a in range(pair)]
        keys = [stacked_heads(new_key, pair * p + a, GROUP) for a in range(pair)]
        lhs.append(
            jnp.concatenate(
                [
                    jnp.concatenate([heads[b] if a == b else blank for b in range(pair)], axis=1)
                    for a in range(pair)
                ],
                axis=0,
            ).astype(jnp.bfloat16)
        )
        own.append(
            jnp.sum(
                jnp.concatenate(heads, axis=0) * jnp.concatenate(keys, axis=0),
                axis=1,
                keepdims=True,
            )
            * scale
        )

    scores = [None] * pairs
    pl.loop(0, rows)(lambda r: load_k(r).wait())
    for r in range(rows):
        for p in range(pairs):
            part = lax.dot_general(
                lhs[p],
                k_ref[r, :, p * wide : (p + 1) * wide],
                (((1,), (1,)), ((), ())),
                preferred_element_type=jnp.float32,
            )
            scores[p] = part if r == 0 else jnp.where(row_of == r, part, scores[p])
    probs, own_probs = [], []
    for p in range(pairs):
        old = jnp.where(live, scores[p] * scale, -1e30)
        top = jnp.maximum(jnp.max(old, axis=1, keepdims=True), own[p])
        e_old = jnp.exp(old - top)
        e_own = jnp.exp(own[p] - top)
        share = 1.0 / (jnp.sum(e_old, axis=1, keepdims=True) + e_own)
        probs.append((e_old * share).astype(jnp.bfloat16))
        own_probs.append((e_own * share).astype(jnp.bfloat16).astype(jnp.float32))
    sums = [None] * pairs
    pl.loop(0, rows)(lambda r: load_v(r).wait())
    for r in range(rows):
        for p in range(pairs):
            part = jnp.dot(
                probs[p],
                v_ref[r, :, p * wide : (p + 1) * wide],
                preferred_element_type=jnp.float32,
            )
            sums[p] = part if r == 0 else jnp.where(row_of == r, part, sums[p])
    power = jnp.zeros((rows, HEAD_DIM), jnp.float32)
    for p in range(pairs):
        for a in range(pair):
            head = pair * p + a
            fresh = stacked_heads(new_value, head, GROUP)
            low = a * stack
            attended = (
                sums[p][low : low + stack, a * HEAD_DIM : (a + 1) * HEAD_DIM]
                + own_probs[p][low : low + stack] * fresh
            )
            for j in range(GROUP):
                at = pl.ds((head * GROUP + j) * HEAD_DIM, HEAD_DIM)
                mixed = res_ref[:, at].astype(jnp.float32) + attended[j * rows : (j + 1) * rows]
                mixed_ref[:, at] = mixed
                power = power + mixed * mixed
    mean = jnp.sum(power, axis=1, keepdims=True) * (1.0 / width)
    normed = mixed_ref[...] * lax.rsqrt(mean + 1e-05) * gain_ref[...].astype(jnp.float32).reshape(1, width)
    normed = normed.astype(jnp.bfloat16).astype(jnp.float32)

    router = router_ref[...].astype(jnp.float32)
    logits = [jnp.sum(normed * router[e : e + 1], axis=1, keepdims=True) for e in range(experts)]
    row_col = lax.broadcasted_iota(jnp.int32, (rows, 1), 0)

    def picked(i):
        value = jnp.zeros((rows, 1), jnp.float32)
        for r in range(rows):
            for e in range(experts):
                value = jnp.where((row_col == r) & (routes[i, r] == e), logits[e], value)
        return value

    first, second = picked(0), picked(1)
    share_of = [1.0 / (1.0 + jnp.exp(second - first)), 1.0 / (1.0 + jnp.exp(first - second))]

    here = lax.axis_index("grp")
    named = [(r, i, routes[i, r]) for r in range(rows) for i in range(2)]
    slots = []
    for at, (r, i, e) in enumerate(named):
        rank = jnp.int32(0)
        for _, _, other in named[:at]:
            rank = rank + (other == e).astype(jnp.int32)
        slots.append(jnp.bitwise_xor(e, here) * most + rank)
    slot_col = lax.broadcasted_iota(jnp.int32, (experts * most, 1), 0)
    slot_row = lax.broadcasted_iota(jnp.int32, (rows, experts * most), 1)
    outgoing = jnp.zeros((experts * most, width), jnp.float32)
    mixing = jnp.zeros((rows, experts * most), jnp.float32)
    for (r, i, _), slot in zip(named, slots, strict=True):
        outgoing = jnp.where(slot_col == slot, normed[r : r + 1], outgoing)
        mixing = jnp.where((slot_row == slot) & (row_col == r), share_of[i], mixing)
    outgoing = outgoing.astype(jnp.bfloat16)
    for j in range(experts):
        out_refs[j][...] = outgoing[j * most : (j + 1) * most]
    mixing_ref[...] = mixing


def load_kernel(first, w_any, _, out_ref, sem):
    load = pltpu.make_async_copy(w_any.at[0, pl.ds(first, out_ref.shape[0])], out_ref, sem)
    load.start()
    load.wait()


def stack_kernel(count, *refs):
    refs[-1][...] = jnp.concatenate(
        [ref[...].astype(jnp.float32) for ref in refs[:count][::-1]], axis=0
    ).astype(jnp.bfloat16)


def experts_kernel(
    own_ref,
    rest_ref,
    core_own_ref,
    core_rest_ref,
    gate_ref,
    up_low_ref,
    up_high_ref,
    down_any,
    keep_ref,
    send_ref,
    x_ref,
    gate_sum,
    up_sum,
    down_ref,
    sems,
):
    chunks = sems.shape[0]
    part = down_ref.shape[0] // chunks

    def load(i):
        at = pl.ds(i * part, part)
        return pltpu.make_async_copy(down_any.at[0, at], down_ref.at[at], sems.at[i])

    pl.loop(0, chunks)(lambda i: load(i).start())
    width = x_ref.shape[1]
    half = keep_ref.shape[0]
    x_ref[:half] = jnp.concatenate([own_ref[...], rest_ref[...]], axis=0)
    x_ref[half:] = jnp.concatenate([core_own_ref[...], core_rest_ref[...]], axis=0)
    first = 0
    for ref in (up_low_ref, up_high_ref):
        tall = ref.shape[0] // 3
        for i in range(3):
            x = x_ref[:, first : first + tall]
            at = pl.ds(i * tall, tall)
            gate = jnp.dot(x, gate_ref[0, pl.ds(first, tall)], preferred_element_type=jnp.float32)
            upper = jnp.dot(x, ref[at], preferred_element_type=jnp.float32)
            gate_sum[...] = gate if first == 0 else gate_sum[...] + gate
            up_sum[...] = upper if first == 0 else up_sum[...] + upper
            first += tall
    gate = gate_sum[...]
    hidden = (gate / (1.0 + jnp.exp(-gate)) * up_sum[...]).astype(jnp.bfloat16)
    pl.loop(0, chunks)(lambda i: load(i).wait())
    deep = 1024
    for step in range(width // deep):
        at = pl.ds(step * deep, deep)
        piece = jnp.dot(hidden, down_ref[:, at], preferred_element_type=jnp.float32)
        piece = piece.astype(jnp.bfloat16)
        keep_ref[:, at] = piece[:half]
        send_ref[:, at] = piece[half:]


def chip_sum_kernel(keep_ref, got_ref, own_ref, *out_refs):
    total = keep_ref[...].astype(jnp.float32) + got_ref[...].astype(jnp.float32)
    part = own_ref.shape[0]
    own_ref[...] = total[:part]
    for i, ref in enumerate(out_refs):
        ref[...] = total[(i + 1) * part : (i + 2) * part].astype(jnp.bfloat16)


def plane_sum_kernel(got, own_ref, *refs):
    total = own_ref[...]
    for ref in refs[:got]:
        total = total + ref[...].astype(jnp.float32)
    total = total.astype(jnp.bfloat16)
    outs = refs[got:]
    most = outs[0].shape[0]
    for j, ref in enumerate(outs):
        ref[...] = total[j * most : (j + 1) * most]


def finish_kernel(*refs):
    *got, mixed_ref, mixing_ref, out_ref = refs
    total = mixed_ref[...]
    most = got[0].shape[0]
    for j, ref in enumerate(got[::-1]):
        rows = ref[...].astype(jnp.float32)
        for s in range(most):
            at = j * most + s
            total = total + mixing_ref[:, at : at + 1] * rows[s : s + 1]
    out_ref[...] = total.astype(jnp.bfloat16)


def call(kernel, outs, in_specs, *args, scratch=(), limit=8, cost=None):
    return pl.pallas_call(
        kernel,
        out_shape=outs,
        in_specs=in_specs,
        out_specs=jax.tree.map(lambda _: VMEM, outs),
        scratch_shapes=list(scratch),
        compiler_params=pltpu.CompilerParams(vmem_limit_bytes=limit * MIB),
        cost_estimate=cost,
    )(*args)


def in_hbm(x):
    return pltpu.with_memory_space_constraint(x, pltpu.HBM)


def shape(extent, kind=jnp.bfloat16):
    return jax.ShapeDtypeStruct(extent, kind)


def local(
    query,
    k_cache,
    v_cache,
    new_key,
    new_value,
    lengths,
    residual,
    norm_gain,
    router,
    routes,
    w_gate,
    w_up,
    w_down,
):
    rows, width = query.shape
    experts = lax.axis_size("grp")
    n_side = lax.axis_size("side")
    n_cuts = lax.axis_size("cuts")
    most = max(2, 2 * rows // experts)
    slots = experts * most
    plane = ("side", "cuts")

    def to_grp(x, j):
        return lax.ppermute(x, "grp", [(i, i ^ j) for i in range(experts)])

    def to_plane(x, k):
        return lax.ppermute(x, plane, [(i, i ^ k) for i in range(n_side * n_cuts)])

    hidden = w_gate.shape[2]

    small = [
        pltpu.make_async_copy(hbm_refs[i], scratch[i], sem.at[i]) for i in range(n_in - 2)
    ]

    def load_k(r):
        return pltpu.make_async_copy(k_any.at[r], k_ref.at[r], cache_sems.at[0, r])

    def load_v(r):
        return pltpu.make_async_copy(v_any.at[r], v_ref.at[r], cache_sems.at[1, r])

    for load in small:
        load.start()

    @pl.loop(0, rows)
    def _(r):
        load_k(r).start()

    @pl.loop(0, rows)
    def _(r):
        load_v(r).start()

    for load in small:
        load.wait()

    pair = 2
    pairs = KV_HEADS // pair
    stack = GROUP * rows
    tall = pair * stack
    wide = pair * HEAD_DIM
    row_of = lax.broadcasted_iota(jnp.int32, (tall, 1), 0) % rows
    length_of = jnp.zeros((tall, 1), jnp.int32)
    for r in range(rows):
        length_of = jnp.where(row_of == r, lengths[r], length_of)
    live = lax.broadcasted_iota(jnp.int32, (tall, span), 1) < length_of

    query = q_ref[...].astype(jnp.float32)
    new_key = nk_ref[...].astype(jnp.float32)
    new_value = nv_ref[...].astype(jnp.float32)
    blank = jnp.zeros((stack, HEAD_DIM), jnp.float32)
    lhs, own = [], []
    for p in range(pairs):
        heads = [stacked_heads(query, (pair * p + a) * GROUP) for a in range(pair)]
        keys = [stacked_heads(new_key, pair * p + a, GROUP) for a in range(pair)]
        lhs.append(
            jnp.concatenate(
                [
                    jnp.concatenate([heads[b] if a == b else blank for b in range(pair)], axis=1)
                    for a in range(pair)
                ],
                axis=0,
            ).astype(jnp.bfloat16)
        )
        own.append(
            jnp.sum(
                jnp.concatenate(heads, axis=0) * jnp.concatenate(keys, axis=0),
                axis=1,
                keepdims=True,
            )
            * scale
        )

    scores = [None] * pairs
    pl.loop(0, rows)(lambda r: load_k(r).wait())
    for r in range(rows):
        for p in range(pairs):
            part = lax.dot_general(
                lhs[p],
                k_ref[r, :, p * wide : (p + 1) * wide],
                (((1,), (1,)), ((), ())),
                preferred_element_type=jnp.float32,
            )
            scores[p] = part if r == 0 else jnp.where(row_of == r, part, scores[p])
    probs, own_probs = [], []
    for p in range(pairs):
        old = jnp.where(live, scores[p] * scale, -1e30)
        top = jnp.maximum(jnp.max(old, axis=1, keepdims=True), own[p])
        e_old = jnp.exp(old - top)
        e_own = jnp.exp(own[p] - top)
        share = 1.0 / (jnp.sum(e_old, axis=1, keepdims=True) + e_own)
        probs.append((e_old * share).astype(jnp.bfloat16))
        own_probs.append((e_own * share).astype(jnp.bfloat16).astype(jnp.float32))
    sums = [None] * pairs
    pl.loop(0, rows)(lambda r: load_v(r).wait())
    for r in range(rows):
        for p in range(pairs):
            part = jnp.dot(
                probs[p],
                v_ref[r, :, p * wide : (p + 1) * wide],
                preferred_element_type=jnp.float32,
            )
            sums[p] = part if r == 0 else jnp.where(row_of == r, part, sums[p])
    power = jnp.zeros((rows, HEAD_DIM), jnp.float32)
    for p in range(pairs):
        for a in range(pair):
            head = pair * p + a
            fresh = stacked_heads(new_value, head, GROUP)
            low = a * stack
            attended = (
                sums[p][low : low + stack, a * HEAD_DIM : (a + 1) * HEAD_DIM]
                + own_probs[p][low : low + stack] * fresh
            )
            for j in range(GROUP):
                at = pl.ds((head * GROUP + j) * HEAD_DIM, HEAD_DIM)
                mixed = res_ref[:, at].astype(jnp.float32) + attended[j * rows : (j + 1) * rows]
                mixed_ref[:, at] = mixed
                power = power + mixed * mixed
    mean = jnp.sum(power, axis=1, keepdims=True) * (1.0 / width)
    normed = mixed_ref[...] * lax.rsqrt(mean + 1e-05) * gain_ref[...].astype(jnp.float32).reshape(1, width)
    normed = normed.astype(jnp.bfloat16).astype(jnp.float32)

    router = router_ref[...].astype(jnp.float32)
    logits = [jnp.sum(normed * router[e : e + 1], axis=1, keepdims=True) for e in range(experts)]
    row_col = lax.broadcasted_iota(jnp.int32, (rows, 1), 0)

    def picked(i):
        value = jnp.zeros((rows, 1), jnp.float32)
        for r in range(rows):
            for e in range(experts):
                value = jnp.where((row_col == r) & (routes[i, r] == e), logits[e], value)
        return value

    first, second = picked(0), picked(1)
    share_of = [1.0 / (1.0 + jnp.exp(second - first)), 1.0 / (1.0 + jnp.exp(first - second))]

    here = lax.axis_index("grp")
    named = [(r, i, routes[i, r]) for r in range(rows) for i in range(2)]
    slots = []
    for at, (r, i, e) in enumerate(named):
        rank = jnp.int32(0)
        for _, _, other in named[:at]:
            rank = rank + (other == e).astype(jnp.int32)
        slots.append(jnp.bitwise_xor(e, here) * most + rank)
    slot_col = lax.broadcasted_iota(jnp.int32, (experts * most, 1), 0)
    slot_row = lax.broadcasted_iota(jnp.int32, (rows, experts * most), 1)
    outgoing = jnp.zeros((experts * most, width), jnp.float32)
    mixing = jnp.zeros((rows, experts * most), jnp.float32)
    for (r, i, _), slot in zip(named, slots, strict=True):
        outgoing = jnp.where(slot_col == slot, normed[r : r + 1], outgoing)
        mixing = jnp.where((slot_row == slot) & (row_col == r), share_of[i], mixing)
    outgoing = outgoing.astype(jnp.bfloat16)
    for j in range(experts):
        out_refs[j][...] = outgoing[j * most : (j + 1) * most]
    mixing_ref[...] = mixing


def load_kernel(first, w_any, _, out_ref, sem):
    load = pltpu.make_async_copy(w_any.at[0, pl.ds(first, out_ref.shape[0])], out_ref, sem)
    load.start()
    load.wait()


def stack_kernel(count, *refs):
    refs[-1][...] = jnp.concatenate(
        [ref[...].astype(jnp.float32) for ref in refs[:count][::-1]], axis=0
    ).astype(jnp.bfloat16)


def experts_kernel(
    own_ref,
    rest_ref,
    core_own_ref,
    core_rest_ref,
    gate_ref,
    up_low_ref,
    up_high_ref,
    down_any,
    keep_ref,
    send_ref,
    x_ref,
    gate_sum,
    up_sum,
    down_ref,
    sems,
):
    chunks = sems.shape[0]
    part = down_ref.shape[0] // chunks

    def load(i):
        at = pl.ds(i * part, part)
        return pltpu.make_async_copy(down_any.at[0, at], down_ref.at[at], sems.at[i])

    pl.loop(0, chunks)(lambda i: load(i).start())
    width = x_ref.shape[1]
    half = keep_ref.shape[0]
    x_ref[:half] = jnp.concatenate([own_ref[...], rest_ref[...]], axis=0)
    x_ref[half:] = jnp.concatenate([core_own_ref[...], core_rest_ref[...]], axis=0)
    first = 0
    for ref in (up_low_ref, up_high_ref):
        tall = ref.shape[0] // 3
        for i in range(3):
            x = x_ref[:, first : first + tall]
            at = pl.ds(i * tall, tall)
            gate = jnp.dot(x, gate_ref[0, pl.ds(first, tall)], preferred_element_type=jnp.float32)
            upper = jnp.dot(x, ref[at], preferred_element_type=jnp.float32)
            gate_sum[...] = gate if first == 0 else gate_sum[...] + gate
            up_sum[...] = upper if first == 0 else up_sum[...] + upper
            first += tall
    gate = gate_sum[...]
    hidden = (gate / (1.0 + jnp.exp(-gate)) * up_sum[...]).astype(jnp.bfloat16)
    pl.loop(0, chunks)(lambda i: load(i).wait())
    deep = 1024
    for step in range(width // deep):
        at = pl.ds(step * deep, deep)
        piece = jnp.dot(hidden, down_ref[:, at], preferred_element_type=jnp.float32)
        piece = piece.astype(jnp.bfloat16)
        keep_ref[:, at] = piece[:half]
        send_ref[:, at] = piece[half:]


def chip_sum_kernel(keep_ref, got_ref, own_ref, *out_refs):
    total = keep_ref[...].astype(jnp.float32) + got_ref[...].astype(jnp.float32)
    part = own_ref.shape[0]
    own_ref[...] = total[:part]
    for i, ref in enumerate(out_refs):
        ref[...] = total[(i + 1) * part : (i + 2) * part].astype(jnp.bfloat16)


def plane_sum_kernel(got, own_ref, *refs):
    total = own_ref[...]
    for ref in refs[:got]:
        total = total + ref[...].astype(jnp.float32)
    total = total.astype(jnp.bfloat16)
    outs = refs[got:]
    most = outs[0].shape[0]
    for j, ref in enumerate(outs):
        ref[...] = total[j * most : (j + 1) * most]


def finish_kernel(*refs):
    *got, mixed_ref, mixing_ref, out_ref = refs
    total = mixed_ref[...]
    most = got[0].shape[0]
    for j, ref in enumerate(got[::-1]):
        rows = ref[...].astype(jnp.float32)
        for s in range(most):
            at = j * most + s
            total = total + mixing_ref[:, at : at + 1] * rows[s : s + 1]
    out_ref[...] = total.astype(jnp.bfloat16)


def call(kernel, outs, in_specs, *args, scratch=(), limit=8, cost=None):
    return pl.pallas_call(
        kernel,
        out_shape=outs,
        in_specs=in_specs,
        out_specs=jax.tree.map(lambda _: VMEM, outs),
        scratch_shapes=list(scratch),
        compiler_params=pltpu.CompilerParams(vmem_limit_bytes=limit * MIB),
        cost_estimate=cost,
    )(*args)


def in_hbm(x):
    return pltpu.with_memory_space_constraint(x, pltpu.HBM)


def shape(extent, kind=jnp.bfloat16):
    return jax.ShapeDtypeStruct(extent, kind)


def local(
    query,
    k_cache,
    v_cache,
    new_key,
    new_value,
    lengths,
    residual,
    norm_gain,
    router,
    routes,
    w_gate,
    w_up,
    w_down,
):
    rows, width = query.shape
    experts = lax.axis_size("grp")
    n_side = lax.axis_size("side")
    n_cuts = lax.axis_size("cuts")
    most = max(2, 2 * rows // experts)
    slots = experts * most
    plane = ("side", "cuts")

    def to_grp(x, j):
        return lax.ppermute(x, "grp", [(i, i ^ j) for i in range(experts)])

    def to_plane(x, k):
        return lax.ppermute(x, plane, [(i, i ^ k) for i in range(n_side * n_cuts)])

    hidden = w_gate.shape[2]

    def weight_piece(count):
        return pltpu.VMEM((count * width // 8, hidden), jnp.bfloat16)

    small = [
        lengths,
        routes.T,
        query,
        new_key,
        new_value,
        residual,
        norm_gain,
        router.T,
    ]
    *outgoing, mixed, mixing = call(
        functools.partial(attend_kernel, experts, most, len(small) + 2),
        [shape((most, width)) for _ in range(experts)]
        + [
            shape((rows, width), jnp.float32),
            shape((rows, slots), jnp.float32),
        ],
        [HBM] * (len(small) + 2),
        *[in_hbm(x) for x in small],
        in_hbm(k_cache),
        in_hbm(v_cache),
        scratch=[
            (pltpu.SMEM if i < 2 else pltpu.VMEM)(x.shape, x.dtype) for i, x in enumerate(small)
        ]
        + [
            pltpu.VMEM(k_cache.shape, jnp.bfloat16),
            pltpu.VMEM(v_cache.shape, jnp.bfloat16),
            pltpu.SemaphoreType.DMA((len(small),)),
            pltpu.SemaphoreType.DMA((2, rows)),
        ],
        limit=14,
    )

    def load(first, after):
        extent = (width // 2, w_up.shape[2])
        return call(
            functools.partial(load_kernel, first),
            pltpu.VMEM(extent, jnp.bfloat16),
            [HBM, ANY],
            in_hbm(w_up),
            after,
            scratch=[pltpu.SemaphoreType.DMA],
            cost=pl.CostEstimate(
                flops=0, bytes_accessed=math.prod(extent) * 2, transcendentals=0
            ),
        )

    up_low = load(0, mixing)
    arrived = [to_grp(outgoing[j], j) for j in range(experts - 1, 0, -1)]
    block = call(
        functools.partial(stack_kernel, experts),
        shape((slots, width)),
        [VMEM] * experts + [ANY],
        *arrived,
        outgoing[0],
        up_low,
        cost=pl.CostEstimate(flops=0, bytes_accessed=16 * MIB, transcendentals=0),
    )
    up_high = load(width // 2, block)
    chips = range(0, n_side * n_cuts, 2)
    others = len(chips) - 1
    fetched = [to_plane(block, k) for k in chips[:0:-1]]
    rest = call(
        functools.partial(stack_kernel, others),
        shape((others * slots, width)),
        [VMEM] * others + [ANY],
        *fetched,
        up_high,
    )
    parts = [block, rest, to_plane(block, 1), to_plane(rest, 1)]
    half = len(chips) * slots
    keep, send = call(
        experts_kernel,
        [shape((half, width))] * 2,
        [VMEM] * 7 + [HBM],
        *parts,
        w_gate,
        up_low,
        up_high,
        in_hbm(w_down),
        scratch=[
            pltpu.VMEM((2 * half, width), jnp.bfloat16),
            pltpu.VMEM((2 * half, hidden), jnp.float32),
            pltpu.VMEM((2 * half, hidden), jnp.float32),
            pltpu.VMEM((hidden, width), jnp.bfloat16),
            pltpu.SemaphoreType.DMA((4,)),
        ],
        limit=28,
    )
    got = to_plane(send, 1)
    own, *partial = call(
        chip_sum_kernel,
        [shape((slots, width), jnp.float32)] + [shape((slots, width))] * others,
        [VMEM] * 2,
        keep,
        got,
    )
    gathered = [to_plane(x, k) for x, k in zip(partial[::-1], chips[:0:-1], strict=True)]
    finished = call(
        functools.partial(plane_sum_kernel, len(gathered)),
        [shape((most, width)) for _ in range(experts)],
        [VMEM] * (1 + len(gathered)),
        own,
        *gathered,
    )
    returned = [to_grp(finished[j], j) for j in range(experts - 1, 0, -1)]
    return call(
        finish_kernel,
        shape((rows, width)),
        [VMEM] * (2 + experts),
        *returned,
        finished[0],
        mixed,
        mixing,
    )


def solution(mesh):
    placed = (
        P(("side", "grp", "cuts"), None),
        P(("side", "grp", "cuts"), None, None),
        P(("side", "grp", "cuts"), None, None),
        P(("side", "grp", "cuts"), None),
        P(("side", "grp", "cuts"), None),
        P(("side", "grp", "cuts")),
        P(("side", "grp", "cuts"), None),
        P(),
        P(),
        P(("side", "grp", "cuts"), None),
        P("grp", None, ("side", "cuts")),
        P("grp", None, ("side", "cuts")),
        P("grp", ("side", "cuts"), None),
    )
    return jax.shard_map(
        local,
        mesh=mesh,
        in_specs=placed,
        out_specs=P(("side", "grp", "cuts"), None),
        check_vma=False,
    )
```

```python
import functools
import math

import jax
import jax.numpy as jnp
from jax import lax
from jax.experimental import pallas as pl
from jax.experimental.pallas import tpu as pltpu
from jax.sharding import PartitionSpec as P

Q_HEADS = 48
KV_HEADS = 8
HEAD_DIM = 128
GROUP = Q_HEADS // KV_HEADS
MIB = 2**20
VMEM = pl.BlockSpec(memory_space=pltpu.VMEM)
SMEM = pl.BlockSpec(memory_space=pltpu.SMEM)
HBM = pl.BlockSpec(memory_space=pltpu.HBM)
ANY = pl.BlockSpec(memory_space=pl.ANY)


def stacked_heads(x, first, copies=1):
    parts = [x[:, (first + j) * HEAD_DIM : (first + j + 1) * HEAD_DIM] for j in range(GROUP // copies)]
    return jnp.concatenate(parts * copies, axis=0)


def attend_kernel(experts, most, n_in, *refs):
    hbm_refs = refs[:n_in]
    out_refs = refs[n_in : n_in + experts]
    mixed_ref, normed_ref = refs[n_in + experts : n_in + experts + 2]
    scratch = refs[n_in + experts + 2 : -2]
    sem, cache_sems = refs[-2:]
    k_any, v_any = hbm_refs[-2:]
    k_ref, v_ref = scratch[-2:]
    lengths, routes, q_ref, nk_ref, nv_ref, res_ref, gain_ref = scratch[:-2]
    rows, width = q_ref.shape
    span = k_ref.shape[1]
    scale = 1.0 / math.sqrt(HEAD_DIM)
    small = [
        pltpu.make_async_copy(hbm_refs[i], scratch[i], sem.at[i]) for i in range(n_in - 2)
    ]

    def load_k(r):
        return pltpu.make_async_copy(k_any.at[r], k_ref.at[r], cache_sems.at[0, r])

    def load_v(r):
        return pltpu.make_async_copy(v_any.at[r], v_ref.at[r], cache_sems.at[1, r])

    for load in small:
        load.start()

    @pl.loop(0, rows)
    def _(r):
        load_k(r).start()

    @pl.loop(0, rows)
    def _(r):
        load_v(r).start()

    for load in small:
        load.wait()

    pair = 2
    pairs = KV_HEADS // pair
    stack = GROUP * rows
    tall = pair * stack
    wide = pair * HEAD_DIM
    row_of = lax.broadcasted_iota(jnp.int32, (tall, 1), 0) % rows
    length_of = jnp.zeros((tall, 1), jnp.int32)
    for r in range(rows):
        length_of = jnp.where(row_of == r, lengths[r], length_of)
    live = lax.broadcasted_iota(jnp.int32, (tall, span), 1) < length_of

    query = q_ref[...].astype(jnp.float32)
    new_key = nk_ref[...].astype(jnp.float32)
    new_value = nv_ref[...].astype(jnp.float32)
    blank = jnp.zeros((stack, HEAD_DIM), jnp.float32)
    lhs, own = [], []
    for p in range(pairs):
        heads = [stacked_heads(query, (pair * p + a) * GROUP) for a in range(pair)]
        keys = [stacked_heads(new_key, pair * p + a, GROUP) for a in range(pair)]
        lhs.append(
            jnp.concatenate(
                [
                    jnp.concatenate([heads[b] if a == b else blank for b in range(pair)], axis=1)
                    for a in range(pair)
                ],
                axis=0,
            ).astype(jnp.bfloat16)
        )
        own.append(
            jnp.sum(
                jnp.concatenate(heads, axis=0) * jnp.concatenate(keys, axis=0),
                axis=1,
                keepdims=True,
            )
            * scale
        )

    scores = [None] * pairs
    pl.loop(0, rows)(lambda r: load_k(r).wait())
    for r in range(rows):
        for p in range(pairs):
            part = lax.dot_general(
                lhs[p],
                k_ref[r, :, p * wide : (p + 1) * wide],
                (((1,), (1,)), ((), ())),
                preferred_element_type=jnp.float32,
            )
            scores[p] = part if r == 0 else jnp.where(row_of == r, part, scores[p])
    probs, own_probs = [], []
    for p in range(pairs):
        old = jnp.where(live, scores[p] * scale, -1e30)
        top = jnp.maximum(jnp.max(old, axis=1, keepdims=True), own[p])
        e_old = jnp.exp(old - top)
        e_own = jnp.exp(own[p] - top)
        share = 1.0 / (jnp.sum(e_old, axis=1, keepdims=True) + e_own)
        probs.append((e_old * share).astype(jnp.bfloat16))
        own_probs.append((e_own * share).astype(jnp.bfloat16).astype(jnp.float32))
    sums = [None] * pairs
    pl.loop(0, rows)(lambda r: load_v(r).wait())
    for r in range(rows):
        for p in range(pairs):
            part = jnp.dot(
                probs[p],
                v_ref[r, :, p * wide : (p + 1) * wide],
                preferred_element_type=jnp.float32,
            )
            sums[p] = part if r == 0 else jnp.where(row_of == r, part, sums[p])
    power = jnp.zeros((rows, HEAD_DIM), jnp.float32)
    for p in range(pairs):
        for a in range(pair):
            head = pair * p + a
            fresh = stacked_heads(new_value, head, GROUP)
            low = a * stack
            attended = (
                sums[p][low : low + stack, a * HEAD_DIM : (a + 1) * HEAD_DIM]
                + own_probs[p][low : low + stack] * fresh
            )
            for j in range(GROUP):
                at = pl.ds((head * GROUP + j) * HEAD_DIM, HEAD_DIM)
                mixed = res_ref[:, at].astype(jnp.float32) + attended[j * rows : (j + 1) * rows]
                mixed_ref[:, at] = mixed
                power = power + mixed * mixed
    mean = jnp.sum(power, axis=1, keepdims=True) * (1.0 / width)
    gain = gain_ref[...].astype(jnp.float32).reshape(1, width)
    normed = (mixed_ref[...] * lax.rsqrt(mean + 1e-05) * gain).astype(jnp.bfloat16)
    normed_ref[...] = normed
    normed = normed.astype(jnp.float32)
    slot_col = lax.broadcasted_iota(jnp.int32, (experts * most, 1), 0)
    outgoing = jnp.zeros((experts * most, width), jnp.float32)
    for r, _, slot in slots_of(routes, rows, most):
        outgoing = jnp.where(slot_col == slot, normed[r : r + 1], outgoing)
    outgoing = outgoing.astype(jnp.bfloat16)
    for j in range(experts):
        out_refs[j][...] = outgoing[j * most : (j + 1) * most]


def slots_of(routes, rows, most):
    here = lax.axis_index("grp")
    named = [(r, i, routes[i, r]) for r in range(rows) for i in range(2)]
    placed = []
    for at, (r, i, e) in enumerate(named):
        rank = jnp.int32(0)
        for _, _, other in named[:at]:
            rank = rank + (other == e).astype(jnp.int32)
        placed.append((r, i, jnp.bitwise_xor(e, here) * most + rank))
    return placed


def mixing_kernel(experts, most, routes, normed_ref, router_ref, mixing_ref):
    rows = normed_ref.shape[0]
    normed = normed_ref[...].astype(jnp.float32)
    router = router_ref[...].astype(jnp.float32)
    logits = [jnp.sum(normed * router[e : e + 1], axis=1, keepdims=True) for e in range(experts)]
    row_col = lax.broadcasted_iota(jnp.int32, (rows, 1), 0)

    def picked(i):
        value = jnp.zeros((rows, 1), jnp.float32)
        for r in range(rows):
            for e in range(experts):
                value = jnp.where((row_col == r) & (routes[i, r] == e), logits[e], value)
        return value

    first, second = picked(0), picked(1)
    share_of = [1.0 / (1.0 + jnp.exp(second - first)), 1.0 / (1.0 + jnp.exp(first - second))]
    slot_row = lax.broadcasted_iota(jnp.int32, (rows, experts * most), 1)
    mixing = jnp.zeros((rows, experts * most), jnp.float32)
    for r, i, slot in slots_of(routes, rows, most):
        mixing = jnp.where((slot_row == slot) & (row_col == r), share_of[i], mixing)
    mixing_ref[...] = mixing


def load_kernel(first, w_any, _, out_ref, sem):
    load = pltpu.make_async_copy(w_any.at[0, pl.ds(first, out_ref.shape[0])], out_ref, sem)
    load.start()
    load.wait()


def stack_kernel(count, *refs):
    refs[-1][...] = jnp.concatenate(
        [ref[...].astype(jnp.float32) for ref in refs[:count]], axis=0
    ).astype(jnp.bfloat16)


def experts_kernel(
    own_ref,
    rest_ref,
    core_own_ref,
    core_rest_ref,
    gate_ref,
    up_low_ref,
    up_high_ref,
    down_any,
    *refs,
):
    *out_refs, x_ref, gate_sum, up_sum, down_ref, sems = refs
    chunks = sems.shape[0]
    part = down_ref.shape[0] // chunks

    def load(i):
        at = pl.ds(i * part, part)
        return pltpu.make_async_copy(down_any.at[0, at], down_ref.at[at], sems.at[i])

    pl.loop(0, chunks)(lambda i: load(i).start())
    width = x_ref.shape[1]
    slots = own_ref.shape[0]
    half = x_ref.shape[0] // 2
    x_ref[:half] = jnp.concatenate([own_ref[...], rest_ref[...]], axis=0)
    x_ref[half:] = jnp.concatenate([core_own_ref[...], core_rest_ref[...]], axis=0)
    first = 0
    tall = up_low_ref.shape[0]
    for ref in (up_low_ref, up_high_ref):
        for i in range(ref.shape[0] // tall):
            x = x_ref[:, first : first + tall]
            at = pl.ds(i * tall, tall)
            gate = jnp.dot(x, gate_ref[0, pl.ds(first, tall)], preferred_element_type=jnp.float32)
            upper = jnp.dot(x, ref[at], preferred_element_type=jnp.float32)
            gate_sum[...] = gate if first == 0 else gate_sum[...] + gate
            up_sum[...] = upper if first == 0 else up_sum[...] + upper
            first += tall
    gate = gate_sum[...]
    hidden = (gate / (1.0 + jnp.exp(-gate)) * up_sum[...]).astype(jnp.bfloat16)
    pl.loop(0, chunks)(lambda i: load(i).wait())
    deep = 1024
    for step in range(width // deep):
        at = pl.ds(step * deep, deep)
        piece = jnp.dot(hidden, down_ref[:, at], preferred_element_type=jnp.float32)
        for i, ref in enumerate(out_refs):
            ref[:, at] = piece[i * slots : (i + 1) * slots].astype(jnp.bfloat16)


def add_kernel(a_ref, b_ref, out_ref):
    total = a_ref[...].astype(jnp.float32) + b_ref[...].astype(jnp.float32)
    out_ref[...] = total.astype(jnp.bfloat16)


def plane_sum_kernel(count, *refs):
    total = refs[0][...].astype(jnp.float32)
    for ref in refs[1:count]:
        total = total + ref[...].astype(jnp.float32)
    total = total.astype(jnp.bfloat16)
    outs = refs[count:]
    most = outs[0].shape[0]
    for j, ref in enumerate(outs):
        ref[...] = total[j * most : (j + 1) * most]


def finish_kernel(*refs):
    *got, mixed_ref, mixing_ref, out_ref = refs
    total = mixed_ref[...]
    most = got[0].shape[0]
    for j, ref in enumerate(got[::-1]):
        rows = ref[...].astype(jnp.float32)
        for s in range(most):
            at = j * most + s
            total = total + mixing_ref[:, at : at + 1] * rows[s : s + 1]
    out_ref[...] = total.astype(jnp.bfloat16)


def call(kernel, outs, in_specs, *args, scratch=(), limit=8, cost=None):
    return pl.pallas_call(
        kernel,
        out_shape=outs,
        in_specs=in_specs,
        out_specs=jax.tree.map(lambda _: VMEM, outs),
        scratch_shapes=list(scratch),
        compiler_params=pltpu.CompilerParams(vmem_limit_bytes=limit * MIB),
        cost_estimate=cost,
    )(*args)


def in_hbm(x):
    return pltpu.with_memory_space_constraint(x, pltpu.HBM)


def shape(extent, kind=jnp.bfloat16):
    return jax.ShapeDtypeStruct(extent, kind)


def local(
    query,
    k_cache,
    v_cache,
    new_key,
    new_value,
    lengths,
    residual,
    norm_gain,
    router,
    routes,
    w_gate,
    w_up,
    w_down,
):
    rows, width = query.shape
    experts = lax.axis_size("grp")
    n_side = lax.axis_size("side")
    n_cuts = lax.axis_size("cuts")
    most = max(2, 2 * rows // experts)
    slots = experts * most
    plane = ("side", "cuts")

    def to_grp(x, j):
        return lax.ppermute(x, "grp", [(i, i ^ j) for i in range(experts)])

    def to_plane(x, k):
        return lax.ppermute(x, plane, [(i, i ^ k) for i in range(n_side * n_cuts)])

    def to_core(x):
        return to_plane(x, 1)

    def stack(*parts, after, cost=None):
        return call(
            functools.partial(stack_kernel, len(parts)),
            shape((sum(x.shape[0] for x in parts), width)),
            [VMEM] * len(parts) + [ANY] * len(after),
            *parts,
            *after,
            cost=cost and pl.CostEstimate(flops=0, bytes_accessed=cost, transcendentals=0),
        )

    small = [
        lengths,
        routes.T,
        query,
        new_key,
        new_value,
        residual,
        norm_gain,
    ]
    *outgoing, mixed, normed = call(
        functools.partial(attend_kernel, experts, most, len(small) + 2),
        [shape((most, width)) for _ in range(experts)]
        + [
            shape((rows, width), jnp.float32),
            shape((rows, width)),
        ],
        [HBM] * (len(small) + 2),
        *[in_hbm(x) for x in small],
        in_hbm(k_cache),
        in_hbm(v_cache),
        scratch=[
            (pltpu.SMEM if i < 2 else pltpu.VMEM)(x.shape, x.dtype) for i, x in enumerate(small)
        ]
        + [
            pltpu.VMEM(k_cache.shape, jnp.bfloat16),
            pltpu.VMEM(v_cache.shape, jnp.bfloat16),
            pltpu.SemaphoreType.DMA((len(small),)),
            pltpu.SemaphoreType.DMA((2, rows)),
        ],
        limit=14,
    )

    def load(first, count, after):
        extent = (count * width // 4, w_up.shape[2])
        return call(
            functools.partial(load_kernel, first * width // 4),
            pltpu.VMEM(extent, jnp.bfloat16),
            [HBM, ANY],
            in_hbm(w_up),
            after,
            scratch=[pltpu.SemaphoreType.DMA],
            cost=pl.CostEstimate(
                flops=0, bytes_accessed=math.prod(extent) * 2, transcendentals=0
            ),
        )

    up_low = load(0, 1, normed)
    mixing = call(
        functools.partial(mixing_kernel, experts, most),
        shape((rows, slots), jnp.float32),
        [SMEM, VMEM, VMEM],
        routes.T,
        normed,
        router.T,
    )
    arrived = [to_grp(outgoing[j], j) for j in range(experts - 1, 0, -1)]
    block = stack(*arrived, outgoing[0], after=[up_low], cost=16 * MIB)
    up_high = load(1, 3, block)
    chips = range(0, n_side * n_cuts, 2)
    core_block = to_core(block)
    fetched = [to_plane(block, k) for k in chips[1:]]
    rest = stack(*fetched, after=[up_high, core_block])
    half = len(chips) * slots
    hidden = w_gate.shape[2]
    outs = call(
        experts_kernel,
        [shape((slots, width))] * (2 * len(chips)),
        [VMEM] * 7 + [HBM],
        block,
        rest,
        core_block,
        to_core(rest),
        w_gate,
        up_low,
        up_high,
        in_hbm(w_down),
        scratch=[
            pltpu.VMEM((2 * half, width), jnp.bfloat16),
            pltpu.VMEM((2 * half, hidden), jnp.float32),
            pltpu.VMEM((2 * half, hidden), jnp.float32),
            pltpu.VMEM((hidden, width), jnp.bfloat16),
            pltpu.SemaphoreType.DMA((4,)),
        ],
        limit=28,
    )
    keep, send = outs[: len(chips)], outs[len(chips) :]
    got = [to_core(x) for x in send[::-1]][::-1]
    sums = [
        call(add_kernel, shape((slots, width)), [VMEM] * 2, keep[i], got[i])
        for i in range(1, len(chips))
    ]
    gathered = [to_plane(x, k) for x, k in zip(sums[::-1], chips[:0:-1], strict=True)]
    *finished, finished_own = call(
        functools.partial(plane_sum_kernel, 2 + len(gathered)),
        [shape((most, width)) for _ in range(experts)],
        [VMEM] * (2 + len(gathered)),
        *gathered,
        keep[0],
        got[0],
    )
    returned = [to_grp(x, experts - 1 - i) for i, x in enumerate(finished)]
    return call(
        finish_kernel,
        shape((rows, width)),
        [VMEM] * (2 + experts),
        *returned,
        finished_own,
        mixed,
        mixing,
    )


def solution(mesh):
    placed = (
        P(("side", "grp", "cuts"), None),
        P(("side", "grp", "cuts"), None, None),
        P(("side", "grp", "cuts"), None, None),
        P(("side", "grp", "cuts"), None),
        P(("side", "grp", "cuts"), None),
        P(("side", "grp", "cuts")),
        P(("side", "grp", "cuts"), None),
        P(),
        P(),
        P(("side", "grp", "cuts"), None),
        P("grp", None, ("side", "cuts")),
        P("grp", None, ("side", "cuts")),
        P("grp", ("side", "cuts"), None),
    )
    return jax.shard_map(
        local,
        mesh=mesh,
        in_specs=placed,
        out_specs=P(("side", "grp", "cuts"), None),
        check_vma=False,
    )
```

```python
import functools
import math

import jax
import jax.numpy as jnp
from jax import lax
from jax.experimental import pallas as pl
from jax.experimental.pallas import tpu as pltpu
from jax.sharding import PartitionSpec as P

Q_HEADS = 48
KV_HEADS = 8
HEAD_DIM = 128
GROUP = Q_HEADS // KV_HEADS
MIB = 2**20
VMEM = pl.BlockSpec(memory_space=pltpu.VMEM)
SMEM = pl.BlockSpec(memory_space=pltpu.SMEM)
HBM = pl.BlockSpec(memory_space=pltpu.HBM)
ANY = pl.BlockSpec(memory_space=pl.ANY)


def stacked_heads(x, first, copies=1):
    parts = [x[:, (first + j) * HEAD_DIM : (first + j + 1) * HEAD_DIM] for j in range(GROUP // copies)]
    return jnp.concatenate(parts * copies, axis=0)


def attend_kernel(experts, most, n_in, *refs):
    hbm_refs = refs[:n_in]
    mixed_ref, power_ref, picks_ref, gain_ref = refs[n_in : n_in + 4]
    scratch = refs[n_in + 4 : -2]
    sem, cache_sems = refs[-2:]
    k_any, v_any = hbm_refs[-2:]
    k_ref, v_ref = scratch[-2:]
    staged = list(scratch[:-2]) + [gain_ref]
    lengths, routes, q_ref, nk_ref, nv_ref, res_ref, _ = staged
    rows, width = q_ref.shape
    span = k_ref.shape[1]
    scale = 1.0 / math.sqrt(HEAD_DIM)
    small = [
        pltpu.make_async_copy(hbm_refs[i], staged[i], sem.at[i]) for i in range(n_in - 2)
    ]

    def load_k(r):
        return pltpu.make_async_copy(k_any.at[r], k_ref.at[r], cache_sems.at[0, r])

    def load_v(r):
        return pltpu.make_async_copy(v_any.at[r], v_ref.at[r], cache_sems.at[1, r])

    @pl.loop(0, rows)
    def _(r):
        load_k(r).start()

    for load in small:
        load.start()

    @pl.loop(0, rows)
    def _(r):
        load_v(r).start()

    for load in small:
        load.wait()

    pair = 2
    pairs = KV_HEADS // pair
    stack = GROUP * rows
    tall = pair * stack
    wide = pair * HEAD_DIM
    row_of = lax.broadcasted_iota(jnp.int32, (tall, 1), 0) % rows
    length_of = jnp.zeros((tall, 1), jnp.int32)
    for r in range(rows):
        length_of = jnp.where(row_of == r, lengths[r], length_of)
    live = lax.broadcasted_iota(jnp.int32, (tall, span), 1) < length_of

    query = q_ref[...].astype(jnp.float32)
    new_key = nk_ref[...].astype(jnp.float32)
    new_value = nv_ref[...].astype(jnp.float32)
    blank = jnp.zeros((stack, HEAD_DIM), jnp.float32)
    lhs, own = [], []
    for p in range(pairs):
        heads = [stacked_heads(query, (pair * p + a) * GROUP) for a in range(pair)]
        keys = [stacked_heads(new_key, pair * p + a, GROUP) for a in range(pair)]
        lhs.append(
            jnp.concatenate(
                [
                    jnp.concatenate([heads[b] if a == b else blank for b in range(pair)], axis=1)
                    for a in range(pair)
                ],
                axis=0,
            ).astype(jnp.bfloat16)
        )
        own.append(
            jnp.sum(
                jnp.concatenate(heads, axis=0) * jnp.concatenate(keys, axis=0),
                axis=1,
                keepdims=True,
            )
            * scale
        )

    scores = [None] * pairs
    pl.loop(0, rows)(lambda r: load_k(r).wait())
    for r in range(rows):
        for p in range(pairs):
            part = lax.dot_general(
                lhs[p],
                k_ref[r, :, p * wide : (p + 1) * wide],
                (((1,), (1,)), ((), ())),
                preferred_element_type=jnp.float32,
            )
            scores[p] = part if r == 0 else jnp.where(row_of == r, part, scores[p])
    probs, own_probs = [], []
    for p in range(pairs):
        old = jnp.where(live, scores[p] * scale, -1e30)
        top = jnp.maximum(jnp.max(old, axis=1, keepdims=True), own[p])
        e_old = jnp.exp(old - top)
        e_own = jnp.exp(own[p] - top)
        share = 1.0 / (jnp.sum(e_old, axis=1, keepdims=True) + e_own)
        probs.append((e_old * share).astype(jnp.bfloat16))
        own_probs.append((e_own * share).astype(jnp.bfloat16).astype(jnp.float32))
    sums = [None] * pairs
    pl.loop(0, rows)(lambda r: load_v(r).wait())
    for r in range(rows):
        for p in range(pairs):
            part = jnp.dot(
                probs[p],
                v_ref[r, :, p * wide : (p + 1) * wide],
                preferred_element_type=jnp.float32,
            )
            sums[p] = part if r == 0 else jnp.where(row_of == r, part, sums[p])
    power = jnp.zeros((rows, HEAD_DIM), jnp.float32)
    for p in range(pairs):
        for a in range(pair):
            head = pair * p + a
            fresh = stacked_heads(new_value, head, GROUP)
            low = a * stack
            attended = (
                sums[p][low : low + stack, a * HEAD_DIM : (a + 1) * HEAD_DIM]
                + own_probs[p][low : low + stack] * fresh
            )
            for j in range(GROUP):
                at = pl.ds((head * GROUP + j) * HEAD_DIM, HEAD_DIM)
                mixed = res_ref[:, at].astype(jnp.float32) + attended[j * rows : (j + 1) * rows]
                mixed_ref[:, at] = mixed
                power = power + mixed * mixed
    power_ref[...] = power
    slot_col = lax.broadcasted_iota(jnp.int32, picks_ref.shape, 0)
    row_col = lax.broadcasted_iota(jnp.int32, picks_ref.shape, 1)
    picks = jnp.zeros(picks_ref.shape, jnp.float32)
    for r, _, slot in slots_of(routes, rows, most):
        picks = jnp.where((slot_col == slot) & (row_col == r), 1.0, picks)
    picks_ref[...] = picks


def norm_kernel(mixed_ref, power_ref, picks_ref, gain_ref, normed_ref, *out_refs):
    rows, width = mixed_ref.shape
    mean = jnp.sum(power_ref[...], axis=1, keepdims=True) * (1.0 / width)
    gain = gain_ref[...].astype(jnp.float32).reshape(1, width)
    normed = (mixed_ref[...] * lax.rsqrt(mean + 1e-05) * gain).astype(jnp.bfloat16)
    normed_ref[...] = normed
    normed = normed.astype(jnp.float32)
    picks = picks_ref[...]
    outgoing = jnp.zeros((picks.shape[0], width), jnp.float32)
    for r in range(rows):
        outgoing = jnp.where(picks[:, r : r + 1] > 0, normed[r : r + 1], outgoing)
    outgoing = outgoing.astype(jnp.bfloat16)
    most = out_refs[0].shape[0]
    for j, ref in enumerate(out_refs):
        ref[...] = outgoing[j * most : (j + 1) * most]


def slots_of(routes, rows, most):
    here = lax.axis_index("grp")
    named = [(r, i, routes[i, r]) for r in range(rows) for i in range(2)]
    placed = []
    for at, (r, i, e) in enumerate(named):
        rank = jnp.int32(0)
        for _, _, other in named[:at]:
            rank = rank + (other == e).astype(jnp.int32)
        placed.append((r, i, jnp.bitwise_xor(e, here) * most + rank))
    return placed


def mixing_kernel(experts, most, routes, normed_ref, router_ref, mixing_ref):
    rows = normed_ref.shape[0]
    normed = normed_ref[...].astype(jnp.float32)
    router = router_ref[...].astype(jnp.float32)
    logits = [jnp.sum(normed * router[e : e + 1], axis=1, keepdims=True) for e in range(experts)]
    row_col = lax.broadcasted_iota(jnp.int32, (rows, 1), 0)

    def picked(i):
        value = jnp.zeros((rows, 1), jnp.float32)
        for r in range(rows):
            for e in range(experts):
                value = jnp.where((row_col == r) & (routes[i, r] == e), logits[e], value)
        return value

    first, second = picked(0), picked(1)
    share_of = [1.0 / (1.0 + jnp.exp(second - first)), 1.0 / (1.0 + jnp.exp(first - second))]
    slot_row = lax.broadcasted_iota(jnp.int32, (rows, experts * most), 1)
    mixing = jnp.zeros((rows, experts * most), jnp.float32)
    for r, i, slot in slots_of(routes, rows, most):
        mixing = jnp.where((slot_row == slot) & (row_col == r), share_of[i], mixing)
    mixing_ref[...] = mixing


def load_kernel(first, w_any, _, out_ref, sem):
    load = pltpu.make_async_copy(w_any.at[0, pl.ds(first, out_ref.shape[0])], out_ref, sem)
    load.start()
    load.wait()


def stack_kernel(count, *refs):
    refs[-1][...] = jnp.concatenate(
        [ref[...].astype(jnp.float32) for ref in refs[:count]], axis=0
    ).astype(jnp.bfloat16)


def experts_kernel(
    own_ref,
    corner_ref,
    sides_ref,
    core_own_ref,
    core_corner_ref,
    core_sides_ref,
    gate_ref,
    up_low_ref,
    up_high_ref,
    down_any,
    *refs,
):
    *out_refs, x_ref, gate_sum, up_sum, down_ref, sems = refs
    chunks = sems.shape[0]
    part = down_ref.shape[0] // chunks

    def load(i):
        at = pl.ds(i * part, part)
        return pltpu.make_async_copy(down_any.at[0, at], down_ref.at[at], sems.at[i])

    pl.loop(0, chunks)(lambda i: load(i).start())
    width = x_ref.shape[1]
    slots = own_ref.shape[0]
    half = x_ref.shape[0] // 2
    x_ref[:half] = jnp.concatenate([own_ref[...], corner_ref[...], sides_ref[...]], axis=0)
    x_ref[half:] = jnp.concatenate(
        [core_own_ref[...], core_corner_ref[...], core_sides_ref[...]], axis=0
    )
    first = 0
    tall = math.gcd(up_low_ref.shape[0], up_high_ref.shape[0])
    for ref in (up_low_ref, up_high_ref):
        for i in range(ref.shape[0] // tall):
            x = x_ref[:, first : first + tall]
            at = pl.ds(i * tall, tall)
            gate = jnp.dot(x, gate_ref[0, pl.ds(first, tall)], preferred_element_type=jnp.float32)
            upper = jnp.dot(x, ref[at], preferred_element_type=jnp.float32)
            gate_sum[...] = gate if first == 0 else gate_sum[...] + gate
            up_sum[...] = upper if first == 0 else up_sum[...] + upper
            first += tall
    gate = gate_sum[...]
    hidden = (gate / (1.0 + jnp.exp(-gate)) * up_sum[...]).astype(jnp.bfloat16)
    pl.loop(0, chunks)(lambda i: load(i).wait())
    deep = 1024
    for step in range(width // deep):
        at = pl.ds(step * deep, deep)
        piece = jnp.dot(hidden, down_ref[:, at], preferred_element_type=jnp.float32)
        for i, ref in enumerate(out_refs):
            ref[:, at] = piece[i * slots : (i + 1) * slots].astype(jnp.bfloat16)


def add_kernel(a_ref, b_ref, out_ref):
    total = a_ref[...].astype(jnp.float32) + b_ref[...].astype(jnp.float32)
    out_ref[...] = total.astype(jnp.bfloat16)


def plane_sum_kernel(count, *refs):
    total = refs[0][...].astype(jnp.float32)
    for ref in refs[1:count]:
        total = total + ref[...].astype(jnp.float32)
    total = total.astype(jnp.bfloat16)
    outs = refs[count:]
    most = outs[0].shape[0]
    for j, ref in enumerate(outs):
        ref[...] = total[j * most : (j + 1) * most]


def finish_kernel(*refs):
    *got, mixed_ref, mixing_ref, out_ref = refs
    total = mixed_ref[...]
    most = got[0].shape[0]
    for j, ref in enumerate(got[::-1]):
        rows = ref[...].astype(jnp.float32)
        for s in range(most):
            at = j * most + s
            total = total + mixing_ref[:, at : at + 1] * rows[s : s + 1]
    out_ref[...] = total.astype(jnp.bfloat16)


def call(kernel, outs, in_specs, *args, scratch=(), limit=8, cost=None):
    return pl.pallas_call(
        kernel,
        out_shape=outs,
        in_specs=in_specs,
        out_specs=jax.tree.map(lambda _: VMEM, outs),
        scratch_shapes=list(scratch),
        compiler_params=pltpu.CompilerParams(vmem_limit_bytes=limit * MIB),
        cost_estimate=cost,
    )(*args)


def in_hbm(x):
    return pltpu.with_memory_space_constraint(x, pltpu.HBM)


def shape(extent, kind=jnp.bfloat16):
    return jax.ShapeDtypeStruct(extent, kind)


def local(
    query,
    k_cache,
    v_cache,
    new_key,
    new_value,
    lengths,
    residual,
    norm_gain,
    router,
    routes,
    w_gate,
    w_up,
    w_down,
):
    rows, width = query.shape
    experts = lax.axis_size("grp")
    n_side = lax.axis_size("side")
    n_cuts = lax.axis_size("cuts")
    most = max(2, 2 * rows // experts)
    slots = experts * most
    plane = ("side", "cuts")

    def to_grp(x, j):
        return lax.ppermute(x, "grp", [(i, i ^ j) for i in range(experts)])

    def to_plane(x, k):
        return lax.ppermute(x, plane, [(i, i ^ k) for i in range(n_side * n_cuts)])

    def to_core(x):
        return to_plane(x, 1)

    def stack(*parts, after):
        return call(
            functools.partial(stack_kernel, len(parts)),
            shape((sum(x.shape[0] for x in parts), width)),
            [VMEM] * len(parts) + [ANY] * len(after),
            *parts,
            *after,
        )

    small = [
        lengths,
        routes.T,
        query,
        new_key,
        new_value,
        residual,
        norm_gain,
    ]
    mixed, power, picks, gain = call(
        functools.partial(attend_kernel, experts, most, len(small) + 2),
        [
            shape((rows, width), jnp.float32),
            shape((rows, HEAD_DIM), jnp.float32),
            shape((slots, rows), jnp.float32),
            shape((width,)),
        ],
        [HBM] * (len(small) + 2),
        *[in_hbm(x) for x in small],
        in_hbm(k_cache),
        in_hbm(v_cache),
        scratch=[
            (pltpu.SMEM if i < 2 else pltpu.VMEM)(x.shape, x.dtype)
            for i, x in enumerate(small[:-1])
        ]
        + [
            pltpu.VMEM(k_cache.shape, jnp.bfloat16),
            pltpu.VMEM(v_cache.shape, jnp.bfloat16),
            pltpu.SemaphoreType.DMA((len(small),)),
            pltpu.SemaphoreType.DMA((2, rows)),
        ],
        limit=14,
    )

    normed, *outgoing = call(
        norm_kernel,
        [shape((rows, width))] + [shape((most, width)) for _ in range(experts)],
        [VMEM] * 4,
        mixed,
        power,
        picks,
        gain,
        cost=pl.CostEstimate(flops=0, bytes_accessed=16 * MIB, transcendentals=0),
    )

    def load(first, count, after):
        extent = (count * width // 4, w_up.shape[2])
        return call(
            functools.partial(load_kernel, first * width // 4),
            pltpu.VMEM(extent, jnp.bfloat16),
            [HBM, ANY],
            in_hbm(w_up),
            after,
            scratch=[pltpu.SemaphoreType.DMA],
        )

    up_low = load(0, 1, normed)
    mixing = call(
        functools.partial(mixing_kernel, experts, most),
        shape((rows, slots), jnp.float32),
        [SMEM, VMEM, VMEM],
        routes.T,
        normed,
        router.T,
    )
    arrived = [to_grp(outgoing[j], j) for j in range(experts - 1, 0, -1)]
    block = stack(*arrived, outgoing[0], after=[up_low])
    up_high = load(1, 3, block)
    chips = range(0, n_side * n_cuts, 2)
    core_block = to_core(block)
    order = [0, chips[-1]] + list(chips[1:-1])
    sides = stack(*[to_plane(block, k) for k in order[2:]], after=[up_high, core_block])
    corner = to_plane(block, order[1])
    half = len(chips) * slots
    hidden = w_gate.shape[2]
    outs = call(
        experts_kernel,
        [shape((slots, width))] * (2 * len(chips)),
        [VMEM] * 9 + [HBM],
        block,
        corner,
        sides,
        core_block,
        to_core(corner),
        to_core(sides),
        w_gate,
        up_low,
        up_high,
        in_hbm(w_down),
        scratch=[
            pltpu.VMEM((2 * half, width), jnp.bfloat16),
            pltpu.VMEM((2 * half, hidden), jnp.float32),
            pltpu.VMEM((2 * half, hidden), jnp.float32),
            pltpu.VMEM((hidden, width), jnp.bfloat16),
            pltpu.SemaphoreType.DMA((4,)),
        ],
        limit=28,
    )
    keep, send = outs[: len(chips)], outs[len(chips) :]
    keep, send = dict(zip(order, keep, strict=True)), dict(zip(order, send, strict=True))
    got = {k: to_core(send[k]) for k in chips[::-1]}
    sums = {
        k: call(add_kernel, shape((slots, width)), [VMEM] * 2, keep[k], got[k])
        for k in chips[:0:-1]
    }
    gathered = [to_plane(sums[k], k) for k in chips[:0:-1]]
    *finished, finished_own = call(
        functools.partial(plane_sum_kernel, 2 + len(gathered)),
        [shape((most, width)) for _ in range(experts)],
        [VMEM] * (2 + len(gathered)),
        *gathered,
        keep[0],
        got[0],
    )
    returned = [to_grp(x, experts - 1 - i) for i, x in enumerate(finished)]
    return call(
        finish_kernel,
        shape((rows, width)),
        [VMEM] * (2 + experts),
        *returned,
        finished_own,
        mixed,
        mixing,
    )


def solution(mesh):
    placed = (
        P(("side", "grp", "cuts"), None),
        P(("side", "grp", "cuts"), None, None),
        P(("side", "grp", "cuts"), None, None),
        P(("side", "grp", "cuts"), None),
        P(("side", "grp", "cuts"), None),
        P(("side", "grp", "cuts")),
        P(("side", "grp", "cuts"), None),
        P(),
        P(),
        P(("side", "grp", "cuts"), None),
        P("grp", None, ("side", "cuts")),
        P("grp", None, ("side", "cuts")),
        P("grp", ("side", "cuts"), None),
    )
    return jax.shard_map(
        local,
        mesh=mesh,
        in_specs=placed,
        out_specs=P(("side", "grp", "cuts"), None),
        check_vma=False,
    )
```

```python
import functools
import math

import jax
import jax.numpy as jnp
from jax import lax
from jax.experimental import pallas as pl
from jax.experimental.pallas import tpu as pltpu
from jax.sharding import PartitionSpec as P

Q_HEADS = 48
KV_HEADS = 8
HEAD_DIM = 128
GROUP = Q_HEADS // KV_HEADS
MIB = 2**20
VMEM = pl.BlockSpec(memory_space=pltpu.VMEM)
SMEM = pl.BlockSpec(memory_space=pltpu.SMEM)
HBM = pl.BlockSpec(memory_space=pltpu.HBM)
ANY = pl.BlockSpec(memory_space=pl.ANY)


def stacked_heads(x, first, copies=1):
    parts = [x[:, (first + j) * HEAD_DIM : (first + j + 1) * HEAD_DIM] for j in range(GROUP // copies)]
    return jnp.concatenate(parts * copies, axis=0)


def attend_kernel(experts, most, n_in, *refs):
    hbm_refs = refs[:n_in]
    mixed_ref, power_ref, picks_ref, gain_ref = refs[n_in : n_in + 4]
    scratch = refs[n_in + 4 : -2]
    sem, cache_sems = refs[-2:]
    k_any, v_any = hbm_refs[-2:]
    k_ref, v_ref = scratch[-2:]
    staged = list(scratch[:-2]) + [gain_ref]
    lengths, routes, q_ref, nk_ref, nv_ref, res_ref, _ = staged
    rows, width = q_ref.shape
    span = k_ref.shape[1]
    scale = 1.0 / math.sqrt(HEAD_DIM)
    small = [
        pltpu.make_async_copy(hbm_refs[i], staged[i], sem.at[i]) for i in range(n_in - 2)
    ]

    def load_k(r):
        return pltpu.make_async_copy(k_any.at[r], k_ref.at[r], cache_sems.at[0, r])

    def load_v(r):
        return pltpu.make_async_copy(v_any.at[r], v_ref.at[r], cache_sems.at[1, r])

    @pl.loop(0, rows)
    def _(r):
        load_k(r).start()

    for load in small:
        load.start()

    @pl.loop(0, rows)
    def _(r):
        load_v(r).start()

    for load in small:
        load.wait()

    pair = 2
    pairs = KV_HEADS // pair
    stack = GROUP * rows
    tall = pair * stack
    wide = pair * HEAD_DIM
    row_of = lax.broadcasted_iota(jnp.int32, (tall, 1), 0) % rows
    length_of = jnp.zeros((tall, 1), jnp.int32)
    for r in range(rows):
        length_of = jnp.where(row_of == r, lengths[r], length_of)
    live = lax.broadcasted_iota(jnp.int32, (tall, span), 1) < length_of

    query = q_ref[...].astype(jnp.float32)
    new_key = nk_ref[...].astype(jnp.float32)
    new_value = nv_ref[...].astype(jnp.float32)
    blank = jnp.zeros((stack, HEAD_DIM), jnp.float32)
    lhs, own = [], []
    for p in range(pairs):
        heads = [stacked_heads(query, (pair * p + a) * GROUP) for a in range(pair)]
        keys = [stacked_heads(new_key, pair * p + a, GROUP) for a in range(pair)]
        lhs.append(
            jnp.concatenate(
                [
                    jnp.concatenate([heads[b] if a == b else blank for b in range(pair)], axis=1)
                    for a in range(pair)
                ],
                axis=0,
            ).astype(jnp.bfloat16)
        )
        own.append(
            jnp.sum(
                jnp.concatenate(heads, axis=0) * jnp.concatenate(keys, axis=0),
                axis=1,
                keepdims=True,
            )
            * scale
        )

    scores = [None] * pairs
    pl.loop(0, rows)(lambda r: load_k(r).wait())
    for r in range(rows):
        for p in range(pairs):
            part = lax.dot_general(
                lhs[p],
                k_ref[r, :, p * wide : (p + 1) * wide],
                (((1,), (1,)), ((), ())),
                preferred_element_type=jnp.float32,
            )
            scores[p] = part if r == 0 else jnp.where(row_of == r, part, scores[p])
    probs, own_probs = [], []
    for p in range(pairs):
        old = jnp.where(live, scores[p] * scale, -1e30)
        top = jnp.maximum(jnp.max(old, axis=1, keepdims=True), own[p])
        e_old = jnp.exp(old - top)
        e_own = jnp.exp(own[p] - top)
        share = 1.0 / (jnp.sum(e_old, axis=1, keepdims=True) + e_own)
        probs.append((e_old * share).astype(jnp.bfloat16))
        own_probs.append((e_own * share).astype(jnp.bfloat16).astype(jnp.float32))
    sums = [None] * pairs
    pl.loop(0, rows)(lambda r: load_v(r).wait())
    for r in range(rows):
        for p in range(pairs):
            part = jnp.dot(
                probs[p],
                v_ref[r, :, p * wide : (p + 1) * wide],
                preferred_element_type=jnp.float32,
            )
            sums[p] = part if r == 0 else jnp.where(row_of == r, part, sums[p])
    power = jnp.zeros((rows, HEAD_DIM), jnp.float32)
    for p in range(pairs):
        for a in range(pair):
            head = pair * p + a
            fresh = stacked_heads(new_value, head, GROUP)
            low = a * stack
            attended = (
                sums[p][low : low + stack, a * HEAD_DIM : (a + 1) * HEAD_DIM]
                + own_probs[p][low : low + stack] * fresh
            )
            for j in range(GROUP):
                at = pl.ds((head * GROUP + j) * HEAD_DIM, HEAD_DIM)
                mixed = res_ref[:, at].astype(jnp.float32) + attended[j * rows : (j + 1) * rows]
                mixed_ref[:, at] = mixed
                power = power + mixed * mixed
    power_ref[...] = power
    slot_col = lax.broadcasted_iota(jnp.int32, picks_ref.shape, 0)
    row_col = lax.broadcasted_iota(jnp.int32, picks_ref.shape, 1)
    picks = jnp.zeros(picks_ref.shape, jnp.float32)
    for r, _, slot in slots_of(routes, rows, most):
        picks = jnp.where((slot_col == slot) & (row_col == r), 1.0, picks)
    picks_ref[...] = picks


def norm_kernel(mixed_ref, power_ref, picks_ref, gain_ref, normed_ref, *out_refs):
    rows, width = mixed_ref.shape
    mean = jnp.sum(power_ref[...], axis=1, keepdims=True) * (1.0 / width)
    gain = gain_ref[...].astype(jnp.float32).reshape(1, width)
    normed = (mixed_ref[...] * lax.rsqrt(mean + 1e-05) * gain).astype(jnp.bfloat16)
    normed_ref[...] = normed
    normed = normed.astype(jnp.float32)
    picks = picks_ref[...]
    outgoing = jnp.zeros((picks.shape[0], width), jnp.float32)
    for r in range(rows):
        outgoing = jnp.where(picks[:, r : r + 1] > 0, normed[r : r + 1], outgoing)
    outgoing = outgoing.astype(jnp.bfloat16)
    most = out_refs[0].shape[0]
    for j, ref in enumerate(out_refs):
        ref[...] = outgoing[j * most : (j + 1) * most]


def slots_of(routes, rows, most):
    here = lax.axis_index("grp")
    named = [(r, i, routes[i, r]) for r in range(rows) for i in range(2)]
    placed = []
    for at, (r, i, e) in enumerate(named):
        rank = jnp.int32(0)
        for _, _, other in named[:at]:
            rank = rank + (other == e).astype(jnp.int32)
        placed.append((r, i, jnp.bitwise_xor(e, here) * most + rank))
    return placed


def mixing_kernel(experts, most, routes, normed_ref, router_ref, mixing_ref):
    rows = normed_ref.shape[0]
    normed = normed_ref[...].astype(jnp.float32)
    router = router_ref[...].astype(jnp.float32)
    logits = [jnp.sum(normed * router[e : e + 1], axis=1, keepdims=True) for e in range(experts)]
    row_col = lax.broadcasted_iota(jnp.int32, (rows, 1), 0)

    def picked(i):
        value = jnp.zeros((rows, 1), jnp.float32)
        for r in range(rows):
            for e in range(experts):
                value = jnp.where((row_col == r) & (routes[i, r] == e), logits[e], value)
        return value

    first, second = picked(0), picked(1)
    share_of = [1.0 / (1.0 + jnp.exp(second - first)), 1.0 / (1.0 + jnp.exp(first - second))]
    slot_row = lax.broadcasted_iota(jnp.int32, (rows, experts * most), 1)
    mixing = jnp.zeros((rows, experts * most), jnp.float32)
    for r, i, slot in slots_of(routes, rows, most):
        mixing = jnp.where((slot_row == slot) & (row_col == r), share_of[i], mixing)
    mixing_ref[...] = mixing


def load_kernel(first, w_any, _, out_ref, sem):
    load = pltpu.make_async_copy(w_any.at[0, pl.ds(first, out_ref.shape[0])], out_ref, sem)
    load.start()
    load.wait()


def stack_kernel(count, *refs):
    refs[-1][...] = jnp.concatenate(
        [ref[...].astype(jnp.float32) for ref in refs[:count]], axis=0
    ).astype(jnp.bfloat16)


def experts_kernel(
    own_ref,
    corner_ref,
    sides_ref,
    core_own_ref,
    core_corner_ref,
    core_sides_ref,
    gate_ref,
    up_low_ref,
    up_high_ref,
    down_any,
    *refs,
):
    *out_refs, x_ref, gate_sum, up_sum, down_ref, sems = refs
    chunks = sems.shape[0]
    part = down_ref.shape[1] // chunks

    def columns(i, low, count):
        return pl.ds(pl.multiple_of(i * part + low, 128), count)

    def load(i):
        at = columns(i, 0, part)
        return pltpu.make_async_copy(down_any.at[0, :, at], down_ref.at[:, at], sems.at[i])

    pl.loop(0, chunks)(lambda i: load(i).start())
    width = x_ref.shape[1]
    slots = own_ref.shape[0]
    half = x_ref.shape[0] // 2
    x_ref[:half] = jnp.concatenate([own_ref[...], corner_ref[...], sides_ref[...]], axis=0)
    x_ref[half:] = jnp.concatenate(
        [core_own_ref[...], core_corner_ref[...], core_sides_ref[...]], axis=0
    )
    first = 0
    tall = math.gcd(up_low_ref.shape[0], up_high_ref.shape[0])
    for ref in (up_low_ref, up_high_ref):
        for i in range(ref.shape[0] // tall):
            x = x_ref[:, first : first + tall]
            at = pl.ds(i * tall, tall)
            gate = jnp.dot(x, gate_ref[0, pl.ds(first, tall)], preferred_element_type=jnp.float32)
            upper = jnp.dot(x, ref[at], preferred_element_type=jnp.float32)
            gate_sum[...] = gate if first == 0 else gate_sum[...] + gate
            up_sum[...] = upper if first == 0 else up_sum[...] + upper
            first += tall
    gate = gate_sum[...]
    hidden = (gate / (1.0 + jnp.exp(-gate)) * up_sum[...]).astype(jnp.bfloat16)
    deep = 1024

    @pl.loop(0, chunks)
    def _(i):
        load(i).wait()
        for low in range(0, part, deep):
            at = columns(i, low, deep)
            piece = jnp.dot(hidden, down_ref[:, at], preferred_element_type=jnp.float32)
            for j, ref in enumerate(out_refs):
                ref[:, at] = piece[j * slots : (j + 1) * slots].astype(jnp.bfloat16)


def add_kernel(a_ref, b_ref, out_ref):
    total = a_ref[...].astype(jnp.float32) + b_ref[...].astype(jnp.float32)
    out_ref[...] = total.astype(jnp.bfloat16)


def plane_sum_kernel(count, *refs):
    total = refs[0][...].astype(jnp.float32)
    for ref in refs[1:count]:
        total = total + ref[...].astype(jnp.float32)
    total = total.astype(jnp.bfloat16)
    outs = refs[count:]
    most = outs[0].shape[0]
    for j, ref in enumerate(outs):
        ref[...] = total[j * most : (j + 1) * most]


def finish_kernel(*refs):
    *got, mixed_ref, mixing_ref, out_ref = refs
    total = mixed_ref[...]
    most = got[0].shape[0]
    for j, ref in enumerate(got[::-1]):
        rows = ref[...].astype(jnp.float32)
        for s in range(most):
            at = j * most + s
            total = total + mixing_ref[:, at : at + 1] * rows[s : s + 1]
    out_ref[...] = total.astype(jnp.bfloat16)


def call(kernel, outs, in_specs, *args, scratch=(), limit=8, cost=None):
    return pl.pallas_call(
        kernel,
        out_shape=outs,
        in_specs=in_specs,
        out_specs=jax.tree.map(lambda _: VMEM, outs),
        scratch_shapes=list(scratch),
        compiler_params=pltpu.CompilerParams(vmem_limit_bytes=limit * MIB),
        cost_estimate=cost,
    )(*args)


def in_hbm(x):
    return pltpu.with_memory_space_constraint(x, pltpu.HBM)


def shape(extent, kind=jnp.bfloat16):
    return jax.ShapeDtypeStruct(extent, kind)


def local(
    query,
    k_cache,
    v_cache,
    new_key,
    new_value,
    lengths,
    residual,
    norm_gain,
    router,
    routes,
    w_gate,
    w_up,
    w_down,
):
    rows, width = query.shape
    experts = lax.axis_size("grp")
    n_side = lax.axis_size("side")
    n_cuts = lax.axis_size("cuts")
    most = max(2, 2 * rows // experts)
    slots = experts * most
    plane = ("side", "cuts")

    def to_grp(x, j):
        return lax.ppermute(x, "grp", [(i, i ^ j) for i in range(experts)])

    def to_plane(x, k):
        return lax.ppermute(x, plane, [(i, i ^ k) for i in range(n_side * n_cuts)])

    def to_core(x):
        return to_plane(x, 1)

    def stack(*parts, after):
        return call(
            functools.partial(stack_kernel, len(parts)),
            shape((sum(x.shape[0] for x in parts), width)),
            [VMEM] * len(parts) + [ANY] * len(after),
            *parts,
            *after,
        )

    small = [
        lengths,
        routes.T,
        query,
        new_key,
        new_value,
        residual,
        norm_gain,
    ]
    mixed, power, picks, gain = call(
        functools.partial(attend_kernel, experts, most, len(small) + 2),
        [
            shape((rows, width), jnp.float32),
            shape((rows, HEAD_DIM), jnp.float32),
            shape((slots, rows), jnp.float32),
            shape((width,)),
        ],
        [HBM] * (len(small) + 2),
        *[in_hbm(x) for x in small],
        in_hbm(k_cache),
        in_hbm(v_cache),
        scratch=[
            (pltpu.SMEM if i < 2 else pltpu.VMEM)(x.shape, x.dtype)
            for i, x in enumerate(small[:-1])
        ]
        + [
            pltpu.VMEM(k_cache.shape, jnp.bfloat16),
            pltpu.VMEM(v_cache.shape, jnp.bfloat16),
            pltpu.SemaphoreType.DMA((len(small),)),
            pltpu.SemaphoreType.DMA((2, rows)),
        ],
        limit=14,
    )

    normed, *outgoing = call(
        norm_kernel,
        [shape((rows, width))] + [shape((most, width)) for _ in range(experts)],
        [VMEM] * 4,
        mixed,
        power,
        picks,
        gain,
        cost=pl.CostEstimate(flops=0, bytes_accessed=16 * MIB, transcendentals=0),
    )

    def load(first, count, after):
        extent = (count * width // 4, w_up.shape[2])
        return call(
            functools.partial(load_kernel, first * width // 4),
            pltpu.VMEM(extent, jnp.bfloat16),
            [HBM, ANY],
            in_hbm(w_up),
            after,
            scratch=[pltpu.SemaphoreType.DMA],
        )

    up_low = load(0, 1, normed)
    mixing = call(
        functools.partial(mixing_kernel, experts, most),
        shape((rows, slots), jnp.float32),
        [SMEM, VMEM, VMEM],
        routes.T,
        normed,
        router.T,
    )
    arrived = [to_grp(outgoing[j], j) for j in range(experts - 1, 0, -1)]
    block = stack(*arrived, outgoing[0], after=[up_low])
    up_high = load(1, 3, block)
    chips = range(0, n_side * n_cuts, 2)
    core_block = to_core(block)
    order = [0, chips[-1]] + list(chips[1:-1])
    sides = stack(*[to_plane(block, k) for k in order[2:]], after=[up_high, core_block])
    corner = to_plane(block, order[1])
    half = len(chips) * slots
    hidden = w_gate.shape[2]
    outs = call(
        experts_kernel,
        [shape((slots, width))] * (2 * len(chips)),
        [VMEM] * 9 + [HBM],
        block,
        corner,
        sides,
        core_block,
        to_core(corner),
        to_core(sides),
        w_gate,
        up_low,
        up_high,
        in_hbm(w_down),
        scratch=[
            pltpu.VMEM((2 * half, width), jnp.bfloat16),
            pltpu.VMEM((2 * half, hidden), jnp.float32),
            pltpu.VMEM((2 * half, hidden), jnp.float32),
            pltpu.VMEM((hidden, width), jnp.bfloat16),
            pltpu.SemaphoreType.DMA((2,)),
        ],
        limit=28,
    )
    keep, send = outs[: len(chips)], outs[len(chips) :]
    keep, send = dict(zip(order, keep, strict=True)), dict(zip(order, send, strict=True))
    got = {k: to_core(send[k]) for k in chips[::-1]}
    sums = {
        k: call(add_kernel, shape((slots, width)), [VMEM] * 2, keep[k], got[k])
        for k in chips[:0:-1]
    }
    gathered = [to_plane(sums[k], k) for k in chips[:0:-1]]
    *finished, finished_own = call(
        functools.partial(plane_sum_kernel, 2 + len(gathered)),
        [shape((most, width)) for _ in range(experts)],
        [VMEM] * (2 + len(gathered)),
        *gathered,
        keep[0],
        got[0],
    )
    returned = [to_grp(x, experts - 1 - i) for i, x in enumerate(finished)]
    return call(
        finish_kernel,
        shape((rows, width)),
        [VMEM] * (2 + experts),
        *returned,
        finished_own,
        mixed,
        mixing,
    )


def solution(mesh):
    placed = (
        P(("side", "grp", "cuts"), None),
        P(("side", "grp", "cuts"), None, None),
        P(("side", "grp", "cuts"), None, None),
        P(("side", "grp", "cuts"), None),
        P(("side", "grp", "cuts"), None),
        P(("side", "grp", "cuts")),
        P(("side", "grp", "cuts"), None),
        P(),
        P(),
        P(("side", "grp", "cuts"), None),
        P("grp", None, ("side", "cuts")),
        P("grp", None, ("side", "cuts")),
        P("grp", ("side", "cuts"), None),
    )
    return jax.shard_map(
        local,
        mesh=mesh,
        in_specs=placed,
        out_specs=P(("side", "grp", "cuts"), None),
        check_vma=False,
    )
```
